256 devices in a mesh: batch: 8 (over x, core), queue: 32 (over y, z).
Axes of the slice: x: 4, y: 4, z: 8, core: 2. Of those that a mesh axis runs over, the one named last changes fastest.
Arguments:
- queries: bfloat16 [8192, 768], P(('batch', 'queue')), may hold values from -6 to 6
- positives: int32 [8192], P(('batch', 'queue')), may hold values from 0 to 131071
- queue: bfloat16 [131072, 768], P('queue'), may hold values from -6 to 6
- pointer: int32 [1], replicated, may hold values from 0 to 131071
- pooled: bfloat16 [4096, 768], P(('batch', 'queue')), may hold values from -6 to 6
- query_projection_weight: float32 [768, 768], P('queue'), may hold values from -0.21875 to 0.21875
- key_weight: float32 [768, 768], P('queue'), may hold values from -0.21875 to 0.21875
Outputs:
- loss: float32 [8192], P(('batch', 'queue'))
- query_grad: float32 [8192, 768], P(('batch', 'queue'))
- new_queue: bfloat16 [131072, 768], P('queue')
- refreshed_key_weight: float32 [768, 768], P('queue')
The draws below stay inside these ranges and needn't reach their ends.
All inputs are finite; a program needn't handle non-finite values.
Results may differ from the reference program's by a relative error of at most 0.0016.
Values may be sent and summed in bfloat16 or wider, within the bound.
A program may use at most 128 MiB of HBM per device.

```python
import math
import jax
import jax.numpy as jnp
from jax import lax

VECTOR_DIM = 768
QUERIES = 8192
QLEN = 131072
NEW = 4096
N_BATCH = 8


def aligned_rows(key):
    quarter = QUERIES // 4
    within = jax.random.randint(jax.random.fold_in(key, 103), (4,), 0, quarter)
    wild_rows = (within + QUERIES // 8) % quarter + jnp.arange(4) * quarter
    wild_signs = jnp.where(jax.random.bernoulli(jax.random.fold_in(key, 105), 0.5, (4, VECTOR_DIM)), 1.0, -1.0)
    return (wild_rows, wild_signs)


def draw_queue(key, part):
    key = jax.random.fold_in(key, 7)
    common = jnp.where(jax.random.bernoulli(jax.random.fold_in(key, 9), 0.5, (VECTOR_DIM,)), 0.3, -0.3)
    base = jnp.clip(0.3 * jax.random.normal(key, (QLEN, VECTOR_DIM), jnp.float32) + common[None, :], -6.0, 6.0)
    return base.astype(jnp.bfloat16)


def draw_queries(key, part):
    wild_rows, wild_signs = aligned_rows(key)
    key = jax.random.fold_in(key, 11)
    base = jnp.clip(0.3 * jax.random.normal(key, (QUERIES, VECTOR_DIM), jnp.float32), -6.0, 6.0)
    base = base.at[wild_rows].set(wild_signs * 6.0)
    return base.astype(jnp.bfloat16)


def touch_ends(result, rng, smallest, top_value):
    longest = result.shape.index(max(result.shape))
    spots = []
    for shift in (0, 1):
        where = [jax.random.randint(jax.random.fold_in(rng, axis), (), 0, length) for axis, length in enumerate(result.shape)]
        where[longest] = (where[longest] + shift) % result.shape[longest]
        spots.append(tuple(where))
    return result.at[spots[0]].set(smallest).at[spots[1]].set(top_value)


def steps_of(stream_key, dims, split, low, top_value):
    factor_of = 1.0
    for axis_at, blocks in split:
        draws = jax.random.uniform(jax.random.fold_in(jax.random.fold_in(stream_key, 6), axis_at), (blocks,), jnp.float32, low / len(split), top_value / len(split))
        factor_of = factor_of * jnp.repeat(jnp.exp(draws), dims[axis_at] // blocks).reshape((-1,) + (1,) * (len(dims) - 1 - axis_at))
    return factor_of


def noise(stream_key, dims, spread, limit, cuts=(), kind=jnp.bfloat16):
    values = spread * jax.random.normal(stream_key, dims, jnp.float32)
    if cuts:
        values = values * steps_of(stream_key, dims, cuts, -0.22, 0.18)
    return jnp.clip(values, -limit, limit).astype(kind)


def setup_inputs(seed: int = 0) -> dict:
    key_list = jax.random.split(jax.random.key(seed), 8)
    return {
        "queries": draw_queries(jax.random.fold_in(key_list[7], 71), 0),
        "positives": touch_ends(jax.random.randint(key_list[1], (QUERIES,), 0, QLEN), jax.random.fold_in(key_list[1], 1), 0, QLEN - 1).astype(jnp.int32),
        "queue": draw_queue(jax.random.fold_in(key_list[7], 71), 0),
        "pointer": jax.random.randint(key_list[3], (1,), 0, QLEN).astype(jnp.int32),
        "pooled": noise(key_list[4], (NEW, VECTOR_DIM), 1.0, 6.0, ((0, 256),)),
        "query_projection_weight": noise(key_list[5], (VECTOR_DIM, VECTOR_DIM), VECTOR_DIM ** -0.5, 0.21875, ((0, 32),), jnp.float32),
        "key_weight": noise(key_list[6], (VECTOR_DIM, VECTOR_DIM), VECTOR_DIM ** -0.5, 0.21875, ((0, 32),), jnp.float32),
    }


sharpness_divisor = 0.05
momentum_rate = 0.9

def block_loss(queue, block_queries, block_pos):
    similarity_multiplier = 1.0 / (sharpness_divisor * math.sqrt(VECTOR_DIM))
    scores = jnp.dot(block_queries, queue.T, preferred_element_type=jnp.float32) * similarity_multiplier
    top = lax.optimization_barrier(jnp.max(scores, axis=1))
    total = lax.optimization_barrier(jnp.sum(jnp.exp(scores - top[:, None]), axis=1))
    positive = jnp.take_along_axis(scores, block_pos[:, None], axis=1)[:, 0]
    loss = jnp.log(total) + top - positive
    probs = (jnp.exp(scores - top[:, None]) / total[:, None]).astype(jnp.bfloat16)
    grad = jnp.dot(probs, queue, preferred_element_type=jnp.float32) - jnp.take(queue, block_pos, axis=0).astype(jnp.float32)
    return (loss, grad * similarity_multiplier)

def reference(queries, positives, queue, pointer, pooled, query_projection_weight, key_weight):
    blocks = QUERIES // N_BATCH
    query_blocks = queries.reshape(N_BATCH, blocks, VECTOR_DIM)
    pos_blocks = positives.reshape(N_BATCH, blocks)
    loss, grad = lax.map(lambda pair: block_loss(queue, pair[0], pair[1]), (query_blocks, pos_blocks))
    loss = loss.reshape(QUERIES)
    query_grad = grad.reshape(QUERIES, VECTOR_DIM)
    refreshed_key_weight = momentum_rate * key_weight + (1.0 - momentum_rate) * query_projection_weight
    keys = jnp.dot(pooled, refreshed_key_weight.astype(jnp.bfloat16), preferred_element_type=jnp.float32).astype(jnp.bfloat16)
    slots = ((pointer[0] + jnp.arange(NEW, dtype=jnp.int32)) % QLEN).astype(jnp.int32)
    new_queue = queue.at[slots].set(keys)
    return (loss, query_grad, new_queue, refreshed_key_weight)
```

```python
import functools
import math

import jax
import jax.numpy as jnp
from jax import lax
from jax.experimental import pallas as pl
from jax.experimental.pallas import tpu as pltpu
from jax.sharding import PartitionSpec as P

F32 = jnp.float32
BF16 = jnp.bfloat16
MESH = pl.DeviceIdType.MESH
NY, NZ = 4, 8
D = 768
HALF = D // 2
KEYS = 4096
ROWS = 256
TILE = 512
SIM = 1.0 / (0.05 * math.sqrt(768))
EXP2 = SIM * math.log2(math.e)
RATE = 0.9


def main_kernel(
    q_in, pool_in, pos_in, wq_in, wk_in, queue,
    loss_o, grad_o, ref_o, nq_o, pool_o, w_o,
    Q, GA, GB, POS, S, ACC, OA, OB, QP, ST, STY, STC, STZ, WC, LC,
    SAR, SAL, RAR, RAL, SBR, SBL, RBR, RBL, TA, YA, TB, SCR, SCL, RCR, RCL,
    ssem, rsem, lsem,
):
    b, k = lax.axis_index("batch"), lax.axis_index("queue")
    y, z = k // NZ, k % NZ
    x, c = b // 2, b % 2
    ids = iter(range(96))

    def zdev(d):
        return (b, y * NZ + (z + d + NZ) % NZ)

    def ydev(d):
        return (b, ((y + d + NY) % NY) * NZ + z)

    def xdev(d):
        return (((x + d + 4) % 4) * 2 + c, k)

    core = (b + 1 - 2 * c, k)

    def rcopy(src, dst, dev):
        i = next(ids)
        return pltpu.make_async_remote_copy(
            src_ref=src, dst_ref=dst, send_sem=ssem.at[i], recv_sem=rsem.at[i],
            device_id=dev, device_id_type=MESH,
        )

    pending = []

    def start(src, dst, dev):
        cp = rcopy(src, dst, dev)
        cp.start()
        pending.append(cp)
        return cp

    load_q = pltpu.make_async_copy(queue, Q, lsem.at[0])
    load_q.start()
    copy_nq = pltpu.make_async_copy(queue, nq_o, lsem.at[1])
    copy_nq.start()

    refreshed = RATE * wk_in[...] + (1.0 - RATE) * wq_in[...]
    ref_o[...] = refreshed
    low = jnp.where(c == 0, refreshed[:, :HALF], refreshed[:, HALF:])
    tail = jnp.concatenate([low[16:24], jnp.zeros((8, HALF), F32)], axis=0)
    GA[y, z, 0:16] = q_in[0:16]
    GA[y, z, 16:32] = pool_in[...]
    GB[y, z, 0:16] = q_in[16:32]
    GB[y, z, 16:32] = jnp.concatenate([low[0:16], tail], axis=1).astype(BF16)
    POS[y, z] = pos_in[...]

    barrier = pltpu.get_barrier_semaphore()
    peers = [zdev(d) for d in range(1, NZ)] + [ydev(d) for d in range(1, NY)]
    peers += [xdev(1), xdev(3), core]
    for dev in peers:
        pl.semaphore_signal(barrier, inc=1, device_id=dev, device_id_type=MESH)
    pl.semaphore_wait(barrier, len(peers))

    pos_y = [start(POS.at[y, z], POS.at[y, z], ydev(d)) for d in (1, 2, 3)]
    a_y = [start(GA.at[y, z], GA.at[y, z], ydev(d)) for d in (1, 3, 2)]

    def zi(d):
        return (z + d + NZ) % NZ

    def yi(d):
        return (y + d + NY) % NY

    def bring(s):
        r, l = zi(1 - s), zi(s - 1)
        if s < 4:
            return (start(GB.at[y, r], GB.at[y, r], zdev(1)),
                    start(GB.at[y, l], GB.at[y, l], zdev(-1)))
        return (start(GB.at[y, r, :, :HALF], GB.at[y, r, :, :HALF], zdev(1)),
                start(GB.at[y, l, :, HALF:], GB.at[y, l, :, HALF:], zdev(-1)))

    def aring(s):
        r, l = zi(1 - s), zi(s - 1)
        if s < 4:
            return (start(GA.at[:, r], GA.at[:, r], zdev(1)),
                    start(GA.at[:, l], GA.at[:, l], zdev(-1)))
        return (start(GA.at[:, r, :, :HALF], GA.at[:, r, :, :HALF], zdev(1)),
                start(GA.at[:, l, :, HALF:], GA.at[:, l, :, HALF:], zdev(-1)))

    def got(pair):
        for cp in pair:
            cp.wait_recv()

    bz = bring(1)
    got(pos_y)
    pos_z = [start(POS.at[:, z], POS.at[:, z], zdev(d)) for d in range(1, NZ)]
    got(a_y)
    az = aring(1)
    got(bz)
    bz = bring(2)
    got(pos_z)
    load_q.wait()

    posf = POS[:, :, 0, :].reshape(NY * NZ, 128).astype(F32)
    post = posf.T - (k * KEYS).astype(F32)

    def positives(p):
        col = jnp.concatenate([post[0:32, 8 * p + j:8 * p + j + 1] for j in range(8)], axis=0)
        for t in range(KEYS // TILE):
            at = lax.broadcasted_iota(jnp.int32, (ROWS, TILE), 1) + t * TILE
            hot = jnp.where(at.astype(F32) == col, 1.0, 0.0).astype(BF16)
            d = jnp.dot(hot, Q[t * TILE:(t + 1) * TILE, :], preferred_element_type=F32)
            if t == 0:
                ACC[...] = d
            else:
                ACC[...] += d
        QP[8 * p:8 * p + 8] = ACC[...].reshape(8, 32, D).astype(BF16)

    positives(0)
    got(bz)
    bz = bring(3)
    got(az)
    az = aring(2)
    positives(1)
    got(bz)
    bz = bring(4)
    got(az)
    az = aring(3)
    positives(2)
    got(bz)
    by = (start(GB.at[y], GB.at[y], ydev(1)), start(GB.at[y], GB.at[y], ydev(-1)))
    got(az)
    az = aring(4)
    positives(3)
    got(by)
    u, d = yi(-1), yi(1)
    by = (start(GB.at[u, :, :, :HALF], GB.at[u, :, :, :HALF], ydev(1)),
          start(GB.at[d, :, :, HALF:], GB.at[d, :, :, HALF:], ydev(-1)))
    got(az)

    mine = GA.at[:, :, 16:32, :]
    own_pool = pltpu.make_async_copy(mine, pool_o.at[b], lsem.at[2])
    own_pool.start()
    px = (start(mine, pool_o.at[b], xdev(1)), start(mine, pool_o.at[b], xdev(-1)))
    cs = [start(mine, pool_o.at[b], core)]
    got(by)
    wmine = GB.at[:, :, 16:32, :]
    own_w = pltpu.make_async_copy(wmine, w_o.at[c], lsem.at[3])
    own_w.start()
    cs.append(start(wmine, w_o.at[c], core))

    lane = lax.broadcasted_iota(jnp.int32, (ROWS, 128), 1)

    def chunk(g, carry):
        X = jnp.concatenate(
            [GA[g, :, 0:16].reshape(128, D), GB[g, :, 0:16].reshape(128, D)], axis=0)
        R = jnp.concatenate(
            [QP[pl.ds(g * 8, 8), 0:16].reshape(128, D), QP[pl.ds(g * 8, 8), 16:32].reshape(128, D)], axis=0)
        ps = jnp.sum(X.astype(F32) * R.astype(F32), axis=1, keepdims=True)
        mx = jnp.full((ROWS, 128), -3e38, F32)
        for t in range(KEYS // TILE):
            s = lax.dot_general(X, Q[t * TILE:(t + 1) * TILE, :], (((1,), (1,)), ((), ())),
                                preferred_element_type=F32)
            S[:, t * TILE:(t + 1) * TILE] = s
            for j in range(TILE // 128):
                mx = jnp.maximum(mx, s[:, j * 128:(j + 1) * 128])
        m = jnp.max(mx, axis=1, keepdims=True)
        total = jnp.zeros((ROWS, 128), F32)
        for t in range(KEYS // TILE):
            e = jnp.exp2((S[:, t * TILE:(t + 1) * TILE] - m) * EXP2)
            for j in range(TILE // 128):
                total = total + e[:, j * 128:(j + 1) * 128]
            d = jnp.dot(e.astype(BF16), Q[t * TILE:(t + 1) * TILE, :], preferred_element_type=F32)
            if t == 0:
                ACC[...] = d
            else:
                ACC[...] += d
        l = jnp.sum(total, axis=1, keepdims=True)
        OA[g] = ACC[0:128].reshape(NZ, 16, D)
        OB[g] = ACC[128:256].reshape(NZ, 16, D)
        cols = jnp.where(lane == 0, m, jnp.where(lane == 1, l, ps))
        ST[:, pl.ds(pl.multiple_of(g * ROWS, ROWS), ROWS)] = cols.T[0:8]
        return carry

    lax.fori_loop(0, 2, chunk, 0)
    got(px)
    left, right = ((x + 3) % 4) * 2 + c, ((x + 1) % 4) * 2 + c
    px = (start(pool_o.at[left, :, :, :, :HALF], pool_o.at[left, :, :, :, :HALF], xdev(1)),
          start(pool_o.at[right, :, :, :, HALF:], pool_o.at[right, :, :, :, HALF:], xdev(-1)))
    cs.append(start(pool_o.at[left], pool_o.at[left], core))
    cs.append(start(pool_o.at[right], pool_o.at[right], core))
    lax.fori_loop(2, 4, chunk, 0)

    def combine(ref, n):
        parts = [ref[i] for i in range(n)]
        top = functools.reduce(jnp.maximum, [p[0:1] for p in parts])
        total = sum(p[1:2] * jnp.exp2((p[0:1] - top) * EXP2) for p in parts)
        positive = sum(p[2:3] for p in parts)
        return top, total, positive

    STY[y] = ST[...]
    sy = [start(ST, STY.at[y], ydev(d)) for d in (1, 2, 3)]
    got(sy)
    top, total, positive = combine(STY, NY)
    STC[...] = jnp.concatenate([top, total, positive, jnp.zeros((5, 1024), F32)], axis=0)
    STZ[z] = STC[...]
    sz = [start(STC, STZ.at[z], zdev(d)) for d in range(1, NZ)]
    got(sz)
    top, total, positive = combine(STZ, NZ)
    w = jnp.exp2((ST[0:1] - top) * EXP2) / total
    loss = jnp.log(total) + (top - positive) * SIM
    LC[...] = jnp.broadcast_to(loss, (128, 1024)).T
    WC[...] = jnp.broadcast_to(w, (128, 1024)).T
    at = pl.multiple_of(y * ROWS + z * 16, 16)
    loss_o[0:16] = LC[pl.ds(at, 16), :]
    loss_o[16:32] = LC[pl.ds(at + 128, 16), :]

    def scale(g, carry):
        base = pl.multiple_of(g * ROWS, ROWS)
        for j in range(D // 128):
            n = slice(j * 128, (j + 1) * 128)
            OA[g, :, :, n] = (OA[g, :, :, n] * WC[pl.ds(base, 128), :].reshape(NZ, 16, 128)
                              - QP[pl.ds(g * 8, 8), 0:16, n].astype(F32))
            OB[g, :, :, n] = (OB[g, :, :, n] * WC[pl.ds(base + 128, 128), :].reshape(NZ, 16, 128)
                              - QP[pl.ds(g * 8, 8), 16:32, n].astype(F32))
        return carry

    lax.fori_loop(0, 4, scale, 0)

    class Ring:
        def __init__(self, n, me, dev, get, sr, sl, rr, rl):
            self.n, self.h, self.me, self.dev, self.get = n, n // 2, me, dev, get
            self.sr, self.sl, self.rr, self.rl = sr, sl, rr, rl
            self.s, self.pair = 0, None

        def step(self):
            n, h = self.n, self.h
            self.s += 1
            s = self.s
            dr, dl = (self.me + h + 1 - s) % n, (self.me + n - h - 1 + s) % n
            sr, sl, rr, rl = (r.at[s - 1] for r in (self.sr, self.sl, self.rr, self.rl))
            if s == 1:
                sr[..., :HALF] = self.get(dr)[..., :HALF]
                sl[..., HALF:] = self.get(dl)[..., HALF:]
                sr, rr = (r.at[..., :HALF] for r in (sr, rr))
                sl, rl = (r.at[..., HALF:] for r in (sl, rl))
            else:
                got(self.pair)
                pr, plf = self.rr.at[s - 2], self.rl.at[s - 2]
                if s == 2:
                    sr[..., :HALF] = self.get(dr)[..., :HALF] + pr[..., :HALF]
                    sr[..., HALF:] = self.get(dr)[..., HALF:]
                    sl[..., :HALF] = self.get(dl)[..., :HALF]
                    sl[..., HALF:] = self.get(dl)[..., HALF:] + plf[..., HALF:]
                else:
                    sr[...] = self.get(dr) + pr[...]
                    sl[...] = self.get(dl) + plf[...]
            self.pair = (start(sr, rr, self.dev(1)), start(sl, rl, self.dev(-1)))

        def end(self):
            got(self.pair)
            return self.get(self.me) + self.rr[self.h - 1] + self.rl[self.h - 1]

    ra = Ring(NZ, z, zdev, lambda d: OA[:, d], SAR, SAL, RAR, RAL)
    rb = Ring(NY, y, ydev, lambda d: OB[d], SBR, SBL, RBR, RBL)
    rc = Ring(NZ, z, zdev, lambda d: TB[d], SCR, SCL, RCR, RCL)
    ra.step()
    rb.step()
    ra.step()
    rb.step()
    ra.step()
    TB[...] = rb.end()
    rc.step()
    ra.step()
    rc.step()
    got(px)
    far = ((x + 2) % 4) * 2 + c
    cs.append(start(pool_o.at[far], pool_o.at[far], core))
    rc.step()
    TA[...] = ra.end()
    YA[y] = TA[y]
    ya = [start(TA.at[yi(d)], YA.at[y], ydev(d)) for d in (1, 2, 3)]
    rc.step()
    grad_o[16:32] = rc.end() * SIM
    got(ya)
    grad_o[0:16] = (YA[0] + YA[1] + YA[2] + YA[3]) * SIM
    got(cs)
    for cp in pending:
        cp.wait_send()
    own_pool.wait()
    own_w.wait()
    copy_nq.wait()


def any_spec():
    return pl.BlockSpec(memory_space=pl.ANY)


def vmem_spec():
    return pl.BlockSpec(memory_space=pltpu.VMEM)


def run_main(queries, pooled, pos, wq, wk, queue):
    n = 96
    z4, y2 = (4, NY, 16, D), (2, NZ, 16, D)
    scratch = [
        pltpu.VMEM((KEYS, D), BF16), pltpu.VMEM((NY, NZ, 32, D), BF16), pltpu.VMEM((NY, NZ, 32, D), BF16),
        pltpu.VMEM((NY, NZ, 8, 128), jnp.int32), pltpu.VMEM((ROWS, KEYS), F32), pltpu.VMEM((ROWS, D), F32),
        pltpu.VMEM((NY, NZ, 16, D), F32), pltpu.VMEM((NY, NZ, 16, D), F32), pltpu.VMEM((32, 32, D), BF16),
        pltpu.VMEM((8, 1024), F32), pltpu.VMEM((NY, 8, 1024), F32), pltpu.VMEM((8, 1024), F32),
        pltpu.VMEM((NZ, 8, 1024), F32), pltpu.VMEM((1024, 128), F32), pltpu.VMEM((1024, 128), F32),
    ]
    scratch += [pltpu.VMEM(z4, F32)] * 4 + [pltpu.VMEM(y2, F32)] * 4
    scratch += [pltpu.VMEM((NY, 16, D), F32)] * 2 + [pltpu.VMEM((NZ, 16, D), F32)]
    scratch += [pltpu.VMEM((4, 16, D), F32)] * 4
    scratch += [pltpu.SemaphoreType.DMA((n,)), pltpu.SemaphoreType.DMA((n,)), pltpu.SemaphoreType.DMA((4,))]
    return pl.pallas_call(
        main_kernel,
        name="retrieval",
        out_shape=[
            jax.ShapeDtypeStruct((32, 128), F32), jax.ShapeDtypeStruct((32, D), F32),
            jax.ShapeDtypeStruct((24, D), F32), jax.ShapeDtypeStruct((KEYS, D), BF16),
            jax.ShapeDtypeStruct((8, NY, NZ, 16, D), BF16), jax.ShapeDtypeStruct((2, NY, NZ, 16, D), BF16),
        ],
        in_specs=[vmem_spec()] * 5 + [any_spec()],
        out_specs=[vmem_spec()] * 3 + [any_spec()] * 3,
        scratch_shapes=scratch,
        compiler_params=pltpu.CompilerParams(
            collective_id=0, has_side_effects=True, vmem_limit_bytes=60 * 2**20),
        cost_estimate=pl.CostEstimate(flops=20 * 10**9, bytes_accessed=32 * 10**6, transcendentals=4 * 10**6),
    )(queries, pooled, pos, wq, wk, queue)


BLK = 256


def enqueue_kernel(shift_ref, pool, w, nq_in, nq, PV, WV, WF, WB, KS, OLD, NEW, sem):
    shift = shift_ref[0]

    @pl.when((shift > -KEYS) & (shift < KEYS))
    def _():
        load_p = pltpu.make_async_copy(pool, PV, sem.at[0])
        load_p.start()
        load_w = pltpu.make_async_copy(w, WV, sem.at[1])
        load_w.start()
        load_w.wait()
        for core in range(2):
            n = slice(core * HALF, (core + 1) * HALF)
            for i in range(32):
                part = WV[core, i].astype(F32)
                WF[24 * i:24 * i + 16, n] = part[:, :HALF]
                WF[24 * i + 16:24 * i + 24, n] = part[0:8, HALF:]
        WB[...] = WF[...].astype(BF16)
        load_p.wait()
        first = jnp.maximum(shift, 0)
        last = jnp.minimum(shift, 0) + KEYS

        def make(i, carry):
            r = pl.multiple_of(i * BLK, BLK)
            keys = jnp.dot(PV[pl.ds(r, BLK), :], WB[...], preferred_element_type=F32)
            KS[pl.ds(r + BLK, BLK), :] = keys.astype(BF16).astype(F32)
            return carry

        lax.fori_loop(first // BLK, (last + BLK - 1) // BLK, make, 0)

        def put(i, carry):
            r = pl.multiple_of(i * BLK, BLK)
            fetch = pltpu.make_async_copy(nq.at[pl.ds(r, BLK), :], OLD, sem.at[2])
            fetch.start()
            fetch.wait()
            at = r + shift
            ok = lax.broadcasted_iota(jnp.int32, (BLK, D), 0) + at
            base = pl.multiple_of((at + BLK) // 8 * 8, 8)
            window = KS[pl.ds(base, BLK + 8), :]
            new = pltpu.roll(window, (BLK + 8) - (at + BLK - base), 0)[:BLK]
            NEW[...] = jnp.where((ok >= 0) & (ok < KEYS), new, OLD[...].astype(F32)).astype(BF16)
            send = pltpu.make_async_copy(NEW, nq.at[pl.ds(r, BLK), :], sem.at[3])
            send.start()
            send.wait()
            return carry

        begin = first - shift
        end = last - shift
        lax.fori_loop(begin // BLK, (end + BLK - 1) // BLK, put, 0)


def run_enqueue(shift, pool, w, nq):
    return pl.pallas_call(
        enqueue_kernel,
        name="enqueue",
        out_shape=jax.ShapeDtypeStruct((KEYS, D), BF16),
        in_specs=[pl.BlockSpec(memory_space=pltpu.SMEM)] + [any_spec()] * 3,
        out_specs=any_spec(),
        scratch_shapes=[
            pltpu.VMEM((KEYS, D), BF16), pltpu.VMEM((2, 32, 16, D), BF16), pltpu.VMEM((D, D), F32),
            pltpu.VMEM((D, D), BF16), pltpu.VMEM((KEYS + 2 * BLK + 8, D), F32), pltpu.VMEM((BLK, D), BF16),
            pltpu.VMEM((BLK, D), BF16), pltpu.SemaphoreType.DMA((4,)),
        ],
        input_output_aliases={3: 0},
        compiler_params=pltpu.CompilerParams(vmem_limit_bytes=60 * 2**20),
    )(shift, pool, w, nq)


def local(queries, positives, queue, pointer, pooled, query_projection_weight, key_weight):
    pos = jnp.broadcast_to(jnp.pad(positives, (0, 96))[None, :], (8, 128))
    loss, grad, refreshed, nq, pool, w = run_main(
        queries, pooled, pos, query_projection_weight, key_weight, queue)
    first_row = lax.axis_index("queue") * KEYS
    shift = (first_row - pointer + KEYS * NY * NZ) % (KEYS * NY * NZ)
    shift = jnp.where(shift >= KEYS, shift - KEYS * NY * NZ, shift)
    new_queue = run_enqueue(shift, pool.reshape(KEYS, D), w.reshape(2, 32, 16, D), nq)
    return loss[:, 0], grad, new_queue, refreshed


def solution(mesh):
    both = P(("batch", "queue"), None)
    one = P("queue", None)
    return jax.shard_map(
        local,
        mesh=mesh,
        in_specs=(both, P(("batch", "queue")), one, P(), both, one, one),
        out_specs=(P(("batch", "queue")), both, one, one),
        check_vma=False,
    )
```

```python
import functools
import math

import jax
import jax.numpy as jnp
from jax import lax
from jax.experimental import pallas as pl
from jax.experimental.pallas import tpu as pltpu
from jax.sharding import PartitionSpec as P

F32 = jnp.float32
BF16 = jnp.bfloat16
MESH = pl.DeviceIdType.MESH
NY, NZ = 4, 8
D = 768
HALF = D // 2
KEYS = 4096
ROWS = 256
TILE = 512
SIM = 1.0 / (0.05 * math.sqrt(768))
EXP2 = SIM * math.log2(math.e)
RATE = 0.9


def main_kernel(
    q_in, pool_in, pos_in, wq_in, wk_in, queue,
    loss_o, grad_o, ref_o, keys_o,
    Q, GA, GB, GP, GW, POSY, POSC, POSZ, XC, S, ACC, OA, OB, QP, WH, WF, WB, KV, PALL,
    SA, SAY, SAC, SAZ, SB, SBY, SBC, SBZ, LS, WC,
    SAR, SAL, RAR, RAL, SBR, SBL, RBR, RBL, TA, YA, TB, SCR, SCL, RCR, RCL,
    ssem, rsem, lsem,
):
    b, k = lax.axis_index("batch"), lax.axis_index("queue")
    y, z = k // NZ, k % NZ
    x, c = b // 2, b % 2
    ids = iter(range(NSEM))

    def zi(d):
        return (z + d + NZ) % NZ

    def yi(d):
        return (y + d + NY) % NY

    def zdev(d):
        return (b, y * NZ + zi(d))

    def ydev(d):
        return (b, yi(d) * NZ + z)

    def xdev(d):
        return (((x + d + 4) % 4) * 2 + c, k)

    core = (b + 1 - 2 * c, k)
    pending = []

    def start(src, dst, dev):
        i = next(ids)
        cp = pltpu.make_async_remote_copy(
            src_ref=src, dst_ref=dst, send_sem=ssem.at[i], recv_sem=rsem.at[i],
            device_id=dev, device_id_type=MESH,
        )
        cp.start()
        pending.append(cp)
        return cp

    def got(group):
        for cp in group:
            cp.wait_recv()

    load_q = pltpu.make_async_copy(queue, Q, lsem.at[0])
    load_q.start()

    refreshed = RATE * wk_in[...] + (1.0 - RATE) * wq_in[...]
    ref_o[...] = refreshed
    low = jnp.where(c == 0, refreshed[:, :HALF], refreshed[:, HALF:])
    tail = jnp.concatenate([low[16:24], jnp.zeros((8, HALF), F32)], axis=0)
    GA[y, z] = q_in[0:16]
    GB[y, z] = q_in[16:32]
    GP[y, z] = pool_in[...]
    GW[y, z] = jnp.concatenate([low[0:16], tail], axis=1).astype(BF16)
    POSY[y] = jnp.zeros((8, 128), jnp.int32)
    POSY[y, 0:1, 0:32] = pos_in[...]

    barrier = pltpu.get_barrier_semaphore()
    peers = [zdev(d) for d in range(1, NZ)] + [ydev(d) for d in range(1, NY)]
    peers += [xdev(1), xdev(3), core]
    for dev in peers:
        pl.semaphore_signal(barrier, inc=1, device_id=dev, device_id_type=MESH)
    pl.semaphore_wait(barrier, len(peers))

    class YFirst:
        def __init__(self, ref):
            self.ref, self.s = ref, 0
            self.cps = [start(ref.at[y, z], ref.at[y, z], ydev(d)) for d in (1, 3, 2)]

        def step(self):
            got(self.cps)
            ref, s = self.ref, self.s + 1
            self.s = s
            r, l = zi(1 - s), zi(s - 1)
            if s < 4:
                self.cps = [start(ref.at[:, r], ref.at[:, r], zdev(1)),
                            start(ref.at[:, l], ref.at[:, l], zdev(-1))]
            else:
                self.cps = [start(ref.at[:, r, :, :HALF], ref.at[:, r, :, :HALF], zdev(1)),
                            start(ref.at[:, l, :, HALF:], ref.at[:, l, :, HALF:], zdev(-1))]

        def end(self):
            got(self.cps)

    class ZFirst:
        def __init__(self, ref):
            self.ref, self.s, self.cps = ref, 0, []
            self.step()

        def step(self):
            got(self.cps)
            ref, s = self.ref, self.s + 1
            self.s = s
            r, l = zi(1 - s), zi(s - 1)
            if s < 4:
                self.cps = [start(ref.at[y, r], ref.at[y, r], zdev(1)),
                            start(ref.at[y, l], ref.at[y, l], zdev(-1))]
            elif s == 4:
                self.cps = [start(ref.at[y, r, :, :HALF], ref.at[y, r, :, :HALF], zdev(1)),
                            start(ref.at[y, l, :, HALF:], ref.at[y, l, :, HALF:], zdev(-1))]
            elif s == 5:
                self.cps = [start(ref.at[y], ref.at[y], ydev(1)), start(ref.at[y], ref.at[y], ydev(-1))]
            else:
                u, d = yi(-1), yi(1)
                self.cps = [start(ref.at[u, :, :, :HALF], ref.at[u, :, :, :HALF], ydev(1)),
                            start(ref.at[d, :, :, HALF:], ref.at[d, :, :, HALF:], ydev(-1))]

        def end(self):
            got(self.cps)

    left, right, far = (((x + d) % 4) * 2 + c for d in (3, 1, 2))
    pieces, passed, cs = [], [], []

    def along_x(*offsets):
        for d in offsets:
            src, dst = GP.at[:, zi(d)], PALL.at[b, :, zi(d)]
            pieces.append((d, start(src, dst, xdev(1)), start(src, dst, xdev(-1))))

    def pass_x(n):
        for _ in range(n):
            d, up, down = pieces.pop(0)
            up.wait_recv()
            down.wait_recv()
            l, r = PALL.at[left, :, zi(d), :, :HALF], PALL.at[right, :, zi(d), :, HALF:]
            passed.append(start(l, l, xdev(1)))
            passed.append(start(r, r, xdev(-1)))

    pos_y = [start(POSY.at[y], POSY.at[y], ydev(d)) for d in (1, 2, 3)]
    ga = YFirst(GA)
    gb = ZFirst(GB)
    gp = YFirst(GP)
    got(pos_y)
    POSC[...] = jnp.zeros((8, 128), jnp.int32)
    for d in range(NY):
        POSC[d:d + 1] = POSY[d, 0:1]
    POSZ[z] = POSC[...]
    pos_z = [start(POSC, POSZ.at[z], zdev(d)) for d in range(1, NZ)]
    ga.step()
    gb.step()
    got(pos_z)
    load_q.wait()

    post = POSZ[...].reshape(64, 128).astype(F32).T - (k * KEYS).astype(F32)

    def positives(p, mid):
        col = jnp.concatenate([post[0:32, 8 * j + p:8 * j + p + 1] for j in range(8)], axis=0)
        for t in range(KEYS // TILE):
            if t == 4:
                for f in mid:
                    f()
            at = lax.broadcasted_iota(jnp.int32, (ROWS, TILE), 1) + t * TILE
            hot = jnp.where(at.astype(F32) == col, 1.0, 0.0).astype(BF16)
            d = jnp.dot(hot, Q[t * TILE:(t + 1) * TILE, :], preferred_element_type=F32)
            if t == 0:
                ACC[...] = d
            else:
                ACC[...] += d
        QP[p] = ACC[...].reshape(8, 32, D).astype(BF16)

    positives(0, [ga.step, gb.step])
    positives(1, [gb.step])
    ga.step()
    positives(2, [gb.step])
    positives(3, [ga.step])

    lane = lax.broadcasted_iota(jnp.int32, (ROWS, 128), 1)

    def scores(parts, mid):
        X = jnp.concatenate([p() for p in parts], axis=0)
        mx = jnp.full((ROWS, 128), -3e38, F32)
        for t in range(KEYS // TILE):
            if t == 4:
                for f in mid:
                    f()
            s = lax.dot_general(X, Q[t * TILE:(t + 1) * TILE, :], (((1,), (1,)), ((), ())),
                                preferred_element_type=F32)
            S[:, t * TILE:(t + 1) * TILE] = s
            for j in range(TILE // 128):
                mx = jnp.maximum(mx, s[:, j * 128:(j + 1) * 128])
        XC[...] = X
        return jnp.max(mx, axis=1, keepdims=True)

    def partial(m, positive_rows, mid):
        total = jnp.zeros((ROWS, 128), F32)
        for t in range(KEYS // TILE):
            if t == 4:
                for f in mid:
                    f()
            e = jnp.exp2((S[:, t * TILE:(t + 1) * TILE] - m) * EXP2)
            for j in range(TILE // 128):
                total = total + e[:, j * 128:(j + 1) * 128]
            d = jnp.dot(e.astype(BF16), Q[t * TILE:(t + 1) * TILE, :], preferred_element_type=F32)
            if t == 0:
                ACC[...] = d
            else:
                ACC[...] += d
        l = jnp.sum(total, axis=1, keepdims=True)
        R = jnp.concatenate([p() for p in positive_rows], axis=0)
        ps = jnp.sum(XC[...].astype(F32) * R.astype(F32), axis=1, keepdims=True)
        return jnp.where(lane == 0, m, jnp.where(lane == 1, l, ps)).T

    def scores_a(zs, mid):
        return scores([lambda d=d: GA[:, zi(d)].reshape(64, D) for d in zs], mid)

    def partial_a(m, zs, mid):
        stats = partial(m, [lambda d=d: QP[:, zi(d), 0:16].reshape(64, D) for d in zs], mid)
        for n, d in enumerate(zs):
            OA[:, zi(d)] = ACC[n * 64:(n + 1) * 64].reshape(NY, 16, D)
            for r in range(3):
                SA[pl.ds(r * NZ + zi(d), 1), 0:64] = stats[r:r + 1, n * 64:(n + 1) * 64]

    def scores_b(ys, mid):
        return scores([lambda d=d: GB[yi(d)].reshape(128, D) for d in ys], mid)

    def partial_b(m, ys, mid):
        stats = partial(m, [lambda d=d: QP[yi(d), :, 16:32].reshape(128, D) for d in ys], mid)
        for n, d in enumerate(ys):
            OB[yi(d)] = ACC[n * 128:(n + 1) * 128].reshape(NZ, 16, D)
            for r in range(3):
                SB[pl.ds(r * NY + yi(d), 1), :] = stats[r:r + 1, n * 128:(n + 1) * 128]

    SA[...] = jnp.zeros_like(SA)
    SB[...] = jnp.zeros_like(SB)
    first_a, second_a = (0, 1, -1, 2), (-2, 3, -3, 4)

    def pool_step(n):
        gp.step()
        if n == 0:
            along_x(0)
        else:
            along_x(n, -n)

    gw = ZFirst(GW)
    m = scores_a(first_a, [lambda: pool_step(0)])
    gb.step()
    gw.step()
    partial_a(m, first_a, [lambda: pool_step(1)])
    ga.end()
    pass_x(1)
    gw.step()
    m = scores_a(second_a, [lambda: pool_step(2)])
    gw.step()
    partial_a(m, second_a, [lambda: pool_step(3)])

    def combine(ref, n, h):
        parts = [ref[i] for i in range(n)]
        top = functools.reduce(jnp.maximum, [p[0:h] for p in parts])
        total = sum(p[h:2 * h] * jnp.exp2((p[0:h] - top) * EXP2) for p in parts)
        positive = sum(p[2 * h:3 * h] for p in parts)
        return top, total, positive

    class Stats:
        def __init__(self, own, ys, mid, zs, h):
            self.own, self.ys, self.mid, self.zs, self.h = own, ys, mid, zs, h
            ys[y] = own[...]
            self.cps = [start(own, ys.at[y], ydev(d)) for d in (1, 2, 3)]

        def step(self):
            got(self.cps)
            h, mid, zs = self.h, self.mid, self.zs
            top, total, positive = combine(self.ys, NY, h)
            mid[0:h], mid[h:2 * h], mid[2 * h:3 * h] = top, total, positive
            zs[z] = mid[...]
            self.cps = [start(mid, zs.at[z], zdev(d)) for d in range(1, NZ)]

        def end(self, row, at):
            got(self.cps)
            h = self.h
            top, total, positive = combine(self.zs, NZ, h)
            w = jnp.exp2((self.own[0:h] - top) * EXP2) / total
            LS[0:h] = jnp.log(total) + (top - positive) * SIM
            for i in range(h):
                WC[i] = jnp.broadcast_to(w[i:i + 1], (128, 128)).T
            return pltpu.roll(jnp.broadcast_to(LS[pl.ds(row, 1), :], (8, 128)), at % 128, 1)[0:1]

    def scale_a(i, carry):
        w = WC[i, 0:64].reshape(NY, 16, 128)
        for j in range(D // 128):
            n = slice(j * 128, (j + 1) * 128)
            OA[:, i, :, n] = OA[:, i, :, n] * w - QP[:, i, 0:16, n].astype(F32)
        return carry

    def scale_b(i, carry):
        w = WC[i].reshape(NZ, 16, 128)
        for j in range(D // 128):
            n = slice(j * 128, (j + 1) * 128)
            OB[i, :, :, n] = OB[i, :, :, n] * w - QP[i, :, 16:32, n].astype(F32)
        return carry

    class Ring:
        def __init__(self, n, me, dev, get, sr, sl, rr, rl):
            self.n, self.h, self.me, self.dev, self.get = n, n // 2, me, dev, get
            self.sr, self.sl, self.rr, self.rl = sr, sl, rr, rl
            self.s, self.pair = 0, None

        def step(self):
            n, h = self.n, self.h
            self.s += 1
            s = self.s
            dr, dl = (self.me + h + 1 - s) % n, (self.me + n - h - 1 + s) % n
            sr, sl, rr, rl = (r.at[s - 1] for r in (self.sr, self.sl, self.rr, self.rl))
            if s == 1:
                sr[..., :HALF] = self.get(dr)[..., :HALF]
                sl[..., HALF:] = self.get(dl)[..., HALF:]
                sr, rr = (r.at[..., :HALF] for r in (sr, rr))
                sl, rl = (r.at[..., HALF:] for r in (sl, rl))
            else:
                got(self.pair)
                pr, plf = self.rr.at[s - 2], self.rl.at[s - 2]
                if s == 2:
                    sr[..., :HALF] = self.get(dr)[..., :HALF] + pr[..., :HALF]
                    sr[..., HALF:] = self.get(dr)[..., HALF:]
                    sl[..., :HALF] = self.get(dl)[..., :HALF]
                    sl[..., HALF:] = self.get(dl)[..., HALF:] + plf[..., HALF:]
                else:
                    sr[...] = self.get(dr) + pr[...]
                    sl[...] = self.get(dl) + plf[...]
            self.pair = (start(sr, rr, self.dev(1)), start(sl, rl, self.dev(-1)))

        def end(self):
            got(self.pair)
            return self.get(self.me) + self.rr[self.h - 1] + self.rl[self.h - 1]

    first_b, second_b = (0, 1), (-1, 2)
    ta = Stats(SA, SAY, SAC, SAZ, NZ)

    gb.end()
    gw.step()
    gp.end()
    along_x(4)
    cs.append(start(GP, PALL.at[b], core))
    m = scores_b(first_b, [ta.step])
    pass_x(2)
    partial_b(m, first_b, [])
    ra = Ring(NZ, z, zdev, lambda d: OA[:, d], SAR, SAL, RAR, RAL)
    loss_o[0:1, 0:16] = ta.end(z, 128 - y * 16)[:, 0:16]
    lax.fori_loop(0, NZ, scale_a, 0)
    ra.step()
    gw.step()
    pass_x(2)
    m = scores_b(second_b, [])
    ra.step()
    pass_x(2)
    partial_b(m, second_b, [])
    tb = Stats(SB, SBY, SBC, SBZ, NY)
    gw.end()
    wcopy = start(GW, WH.at[c], core)
    pass_x(1)
    tb.step()

    wcopy.wait_recv()

    def unpack(i, carry):
        own = GW[i // NZ, i % NZ].astype(F32)
        other = WH[1 - c, i // NZ, i % NZ].astype(F32)
        at = pl.multiple_of(i * 24, 8)
        for h in range(2):
            part = jnp.where(c == h, own, other)
            n = slice(h * HALF, (h + 1) * HALF)
            WF[pl.ds(at, 16), n] = part[:, :HALF]
            WF[pl.ds(at + 16, 8), n] = part[0:8, HALF:]
        return carry

    lax.fori_loop(0, NY * NZ, unpack, 0)
    WB[...] = WF[...].astype(BF16)
    ra.step()
    loss_o[0:1, 16:32] = tb.end(y, 144 - z * 16)[:, 16:32]
    lax.fori_loop(0, NY, scale_b, 0)
    rb = Ring(NY, y, ydev, lambda d: OB[d], SBR, SBL, RBR, RBL)
    rb.step()
    own_pool = pltpu.make_async_copy(GP, PALL.at[b], lsem.at[1])
    own_pool.start()
    got(passed)
    cs.extend(start(PALL.at[p], PALL.at[p], core) for p in (left, right, far))
    ra.step()
    rb.step()
    own_pool.wait()
    got(cs)

    def keys(i, carry):
        for p in range(NY):
            KV[i, p * 128:(p + 1) * 128, :] = jnp.dot(
                PALL[i, p].reshape(128, D), WB[...], preferred_element_type=F32).astype(BF16)
        return carry

    lax.fori_loop(0, 6, keys, 0)
    TA[...] = ra.end()
    YA[y] = TA[y]
    ya = [start(TA.at[yi(d)], YA.at[y], ydev(d)) for d in (1, 2, 3)]
    lax.fori_loop(6, 8, keys, 0)
    out_keys = pltpu.make_async_copy(KV, keys_o, lsem.at[1])
    out_keys.start()
    got(ya)
    grad_o[0:16] = (YA[0] + YA[1] + YA[2] + YA[3]) * SIM
    TB[...] = rb.end()
    rc = Ring(NZ, z, zdev, lambda d: TB[d], SCR, SCL, RCR, RCL)
    rc.step()
    rc.step()
    rc.step()
    rc.step()
    grad_o[16:32] = rc.end() * SIM
    for cp in pending:
        cp.wait_send()
    out_keys.wait()


def any_spec():
    return pl.BlockSpec(memory_space=pl.ANY)


def vmem_spec():
    return pl.BlockSpec(memory_space=pltpu.VMEM)


NSEM = 160


def run_main(queries, pooled, pos, wq, wk, queue):
    z4, y2 = (4, NY, 16, D), (2, NZ, 16, D)
    grid = (NY, NZ, 16, D)
    scratch = [pltpu.VMEM((KEYS, D), BF16)] + [pltpu.VMEM(grid, BF16)] * 4
    scratch += [
        pltpu.VMEM((NY, 8, 128), jnp.int32), pltpu.VMEM((8, 128), jnp.int32), pltpu.VMEM((NZ, 8, 128), jnp.int32),
        pltpu.VMEM((ROWS, D), BF16), pltpu.VMEM((ROWS, KEYS), F32),
        pltpu.VMEM((ROWS, D), F32), pltpu.VMEM(grid, F32), pltpu.VMEM(grid, F32),
        pltpu.VMEM((NY, NZ, 32, D), BF16), pltpu.VMEM((2,) + grid, BF16), pltpu.VMEM((D, D), F32),
        pltpu.VMEM((D, D), BF16), pltpu.VMEM((8, 512, D), BF16), pltpu.VMEM((8,) + grid, BF16),
        pltpu.VMEM((24, 128), F32), pltpu.VMEM((NY, 24, 128), F32), pltpu.VMEM((24, 128), F32),
        pltpu.VMEM((NZ, 24, 128), F32), pltpu.VMEM((16, 128), F32), pltpu.VMEM((NY, 16, 128), F32),
        pltpu.VMEM((16, 128), F32), pltpu.VMEM((NZ, 16, 128), F32),
        pltpu.VMEM((8, 128), F32), pltpu.VMEM((8, 128, 128), F32),
    ]
    scratch += [pltpu.VMEM(z4, F32)] * 4 + [pltpu.VMEM(y2, F32)] * 4
    scratch += [pltpu.VMEM((NY, 16, D), F32)] * 2 + [pltpu.VMEM((NZ, 16, D), F32)]
    scratch += [pltpu.VMEM((4, 16, D), F32)] * 4
    scratch += [pltpu.SemaphoreType.DMA((NSEM,)), pltpu.SemaphoreType.DMA((NSEM,)), pltpu.SemaphoreType.DMA((2,))]
    return pl.pallas_call(
        main_kernel,
        name="retrieval",
        out_shape=[
            jax.ShapeDtypeStruct((1, 32), F32), jax.ShapeDtypeStruct((32, D), F32),
            jax.ShapeDtypeStruct((24, D), F32), jax.ShapeDtypeStruct((8, 512, D), BF16),
        ],
        in_specs=[vmem_spec()] * 5 + [any_spec()],
        out_specs=[vmem_spec()] * 3 + [any_spec()],
        scratch_shapes=scratch,
        compiler_params=pltpu.CompilerParams(
            collective_id=0, has_side_effects=True, vmem_limit_bytes=60 * 2**20),
        cost_estimate=pl.CostEstimate(flops=20 * 10**9, bytes_accessed=32 * 10**6, transcendentals=4 * 10**6),
    )(queries, pooled, pos, wq, wk, queue)


BLK = 512
WIN = BLK + 16


def enqueue_kernel(shift_ref, queue, keys, nq, BUF, WV, isem, osem, ksem):
    shift = shift_ref[0]
    steps = KEYS // BLK

    def block(i):
        rows = pl.ds(i * BLK, BLK)
        at = i * BLK + shift
        base = pl.multiple_of(jnp.clip(at // 16 * 16, 0, KEYS - WIN), 16)
        return (at, base, (at > -BLK) & (at < KEYS),
                pltpu.make_async_copy(queue.at[rows, :], BUF.at[i], isem.at[i]),
                pltpu.make_async_copy(BUF.at[i], nq.at[rows, :], osem.at[i]),
                pltpu.make_async_copy(keys.at[pl.ds(base, WIN), :], WV.at[i], ksem.at[i]))

    for i in range(steps):
        _, _, lands, load, _, fetch = block(i)
        load.start()

        @pl.when(lands)
        def _():
            fetch.start()

    for i in range(steps):
        at, base, lands, load, store, fetch = block(i)
        load.wait()

        @pl.when(lands)
        def _():
            fetch.wait()
            new = pltpu.roll(WV[i].astype(F32), (2 * WIN + base - at) % WIN, 0)[:BLK]
            row = lax.broadcasted_iota(jnp.int32, (BLK, 1), 0) + at
            ok = (row >= 0) & (row < KEYS)
            BUF[i] = jnp.where(ok, new, BUF[i].astype(F32)).astype(BF16)

        store.start()
    for i in range(steps):
        block(i)[4].wait()


def run_enqueue(shift, queue, keys):
    steps = KEYS // BLK
    return pl.pallas_call(
        enqueue_kernel,
        name="enqueue",
        out_shape=jax.ShapeDtypeStruct((KEYS, D), BF16),
        in_specs=[pl.BlockSpec(memory_space=pltpu.SMEM)] + [any_spec()] * 2,
        out_specs=any_spec(),
        scratch_shapes=[pltpu.VMEM((steps, BLK, D), BF16), pltpu.VMEM((steps, WIN, D), BF16)]
        + [pltpu.SemaphoreType.DMA((steps,))] * 3,
        compiler_params=pltpu.CompilerParams(vmem_limit_bytes=60 * 2**20),
    )(shift, queue, keys)


def local(queries, positives, queue, pointer, pooled, query_projection_weight, key_weight):
    loss, grad, refreshed, keys = run_main(
        queries, pooled, positives.reshape(1, 32), query_projection_weight, key_weight, queue)
    first_row = lax.axis_index("queue") * KEYS
    shift = (first_row - pointer + KEYS * NY * NZ) % (KEYS * NY * NZ)
    shift = jnp.where(shift >= KEYS, shift - KEYS * NY * NZ, shift)
    new_queue = run_enqueue(shift, queue, keys.reshape(KEYS, D))
    return loss.reshape(32), grad, new_queue, refreshed


def solution(mesh):
    both = P(("batch", "queue"), None)
    one = P("queue", None)
    return jax.shard_map(
        local,
        mesh=mesh,
        in_specs=(both, P(("batch", "queue")), one, P(), both, one, one),
        out_specs=(P(("batch", "queue")), both, one, one),
        check_vma=False,
    )
```

```python
import functools
import math

import jax
import jax.numpy as jnp
from jax import lax
from jax.experimental import pallas as pl
from jax.experimental.pallas import tpu as pltpu
from jax.sharding import PartitionSpec as P

F32 = jnp.float32
BF16 = jnp.bfloat16
MESH = pl.DeviceIdType.MESH
NY, NZ = 4, 8
D = 768
HALF = D // 2
KEYS = 4096
ROWS = 256
TILE = 512
SIM = 1.0 / (0.05 * math.sqrt(768))
EXP2 = SIM * math.log2(math.e)
RATE = 0.9


def main_kernel(
    q_in, pool_in, pos_in, wq_in, wk_in, queue,
    loss_o, grad_o, ref_o, keys_o,
    Q, GA, GB, GP, GW, POSY, POSC, POSZ, XC, S, ACC, OA, OB, QP, WH, WF, WB, KV, PALL,
    SA, SAY, SAC, SAZ, SB, SBY, SBC, SBZ, LS, WC,
    SAR, SAL, RAR, RAL, SBR, SBL, RBR, RBL, TA, YA, TB, SCR, SCL, RCR, RCL,
    ssem, rsem, lsem,
):
    b, k = lax.axis_index("batch"), lax.axis_index("queue")
    y, z = k // NZ, k % NZ
    x, c = b // 2, b % 2
    ids = iter(range(NSEM))

    def zi(d):
        return (z + d + NZ) % NZ

    def yi(d):
        return (y + d + NY) % NY

    def zdev(d):
        return (b, y * NZ + zi(d))

    def ydev(d):
        return (b, yi(d) * NZ + z)

    def xdev(d):
        return (((x + d + 4) % 4) * 2 + c, k)

    core = (b + 1 - 2 * c, k)
    pending = []

    def start(src, dst, dev):
        i = next(ids)
        cp = pltpu.make_async_remote_copy(
            src_ref=src, dst_ref=dst, send_sem=ssem.at[i], recv_sem=rsem.at[i],
            device_id=dev, device_id_type=MESH,
        )
        cp.start()
        pending.append(cp)
        return cp

    def got(group):
        for cp in group:
            cp.wait_recv()

    load_q = pltpu.make_async_copy(queue, Q, lsem.at[0])
    load_q.start()

    refreshed = RATE * wk_in[...] + (1.0 - RATE) * wq_in[...]
    ref_o[...] = refreshed
    low = jnp.where(c == 0, refreshed[:, :HALF], refreshed[:, HALF:])
    tail = jnp.concatenate([low[16:24], jnp.zeros((8, HALF), F32)], axis=0)
    GA[y, z] = q_in[0:16]
    GB[y, z] = q_in[16:32]
    GP[y, z] = pool_in[...]
    GW[y, z] = jnp.concatenate([low[0:16], tail], axis=1).astype(BF16)
    POSY[y] = jnp.zeros((8, 128), jnp.int32)
    POSY[y, 0:1, 0:32] = pos_in[...]

    barrier = pltpu.get_barrier_semaphore()
    peers = [zdev(d) for d in range(1, NZ)] + [ydev(d) for d in range(1, NY)]
    peers += [xdev(1), xdev(3), core]
    for dev in peers:
        pl.semaphore_signal(barrier, inc=1, device_id=dev, device_id_type=MESH)
    pl.semaphore_wait(barrier, len(peers))

    class YFirst:
        def __init__(self, ref):
            self.ref, self.s = ref, 0
            self.cps = [start(ref.at[y, z], ref.at[y, z], ydev(d)) for d in (1, 3, 2)]

        def step(self):
            got(self.cps)
            ref, s = self.ref, self.s + 1
            self.s = s
            r, l = zi(1 - s), zi(s - 1)
            if s < 4:
                self.cps = [start(ref.at[:, r], ref.at[:, r], zdev(1)),
                            start(ref.at[:, l], ref.at[:, l], zdev(-1))]
            else:
                self.cps = [start(ref.at[:, r, :, :HALF], ref.at[:, r, :, :HALF], zdev(1)),
                            start(ref.at[:, l, :, HALF:], ref.at[:, l, :, HALF:], zdev(-1))]

        def end(self):
            got(self.cps)

    class ZFirst:
        def __init__(self, ref):
            self.ref, self.s, self.cps = ref, 0, []
            self.step()

        def step(self):
            got(self.cps)
            ref, s = self.ref, self.s + 1
            self.s = s
            r, l = zi(1 - s), zi(s - 1)
            if s < 4:
                self.cps = [start(ref.at[y, r], ref.at[y, r], zdev(1)),
                            start(ref.at[y, l], ref.at[y, l], zdev(-1))]
            elif s == 4:
                self.cps = [start(ref.at[y, r, :, :HALF], ref.at[y, r, :, :HALF], zdev(1)),
                            start(ref.at[y, l, :, HALF:], ref.at[y, l, :, HALF:], zdev(-1))]
            elif s == 5:
                self.cps = [start(ref.at[y], ref.at[y], ydev(1)), start(ref.at[y], ref.at[y], ydev(-1))]
            else:
                u, d = yi(-1), yi(1)
                self.cps = [start(ref.at[u, :, :, :HALF], ref.at[u, :, :, :HALF], ydev(1)),
                            start(ref.at[d, :, :, HALF:], ref.at[d, :, :, HALF:], ydev(-1))]

        def end(self):
            got(self.cps)

    left, right, far = (((x + d) % 4) * 2 + c for d in (3, 1, 2))
    pieces, passed, cs = [], [], []

    def along_x(*offsets):
        for d in offsets:
            src, dst = GP.at[:, zi(d)], PALL.at[b, :, zi(d)]
            pieces.append((d, start(src, dst, xdev(1)), start(src, dst, xdev(-1))))

    def pass_x(n):
        for _ in range(n):
            d, up, down = pieces.pop(0)
            up.wait_recv()
            down.wait_recv()
            l, r = PALL.at[left, :, zi(d), :, :HALF], PALL.at[right, :, zi(d), :, HALF:]
            passed.append(start(l, l, xdev(1)))
            passed.append(start(r, r, xdev(-1)))

    pos_y = [start(POSY.at[y], POSY.at[y], ydev(d)) for d in (1, 2, 3)]
    gb = ZFirst(GB)
    ga = YFirst(GA)
    gp = YFirst(GP)
    got(pos_y)
    POSC[...] = jnp.zeros((8, 128), jnp.int32)
    for d in range(NY):
        POSC[d:d + 1] = POSY[d, 0:1]
    POSZ[z] = POSC[...]
    pos_z = [start(POSC, POSZ.at[z], zdev(d)) for d in range(1, NZ)]
    gb.step()
    ga.step()
    got(pos_z)
    load_q.wait()

    post = POSZ[...].reshape(64, 128).astype(F32).T - (k * KEYS).astype(F32)

    def positives(p, mid):
        col = jnp.concatenate([post[0:32, 8 * j + p:8 * j + p + 1] for j in range(8)], axis=0)
        for t in range(KEYS // TILE):
            if t == 4:
                for f in mid:
                    f()
            at = lax.broadcasted_iota(jnp.int32, (ROWS, TILE), 1) + t * TILE
            hot = jnp.where(at.astype(F32) == col, 1.0, 0.0).astype(BF16)
            d = jnp.dot(hot, Q[t * TILE:(t + 1) * TILE, :], preferred_element_type=F32)
            if t == 0:
                ACC[...] = d
            else:
                ACC[...] += d
        QP[p] = ACC[...].reshape(8, 32, D).astype(BF16)

    def pool_step(n):
        gp.step()
        if n == 0:
            along_x(0)
        else:
            along_x(n, -n)

    positives(0, [gb.step])
    gb.step()
    pool_step(0)
    positives(1, [ga.step])
    gb.step()
    positives(2, [lambda: pool_step(1)])
    ga.step()
    positives(3, [])

    lane = lax.broadcasted_iota(jnp.int32, (ROWS, 128), 1)

    def scores(parts, mid):
        X = jnp.concatenate([p() for p in parts], axis=0)
        mx = jnp.full((ROWS, 128), -3e38, F32)
        for t in range(KEYS // TILE):
            if t == 4:
                for f in mid:
                    f()
            s = lax.dot_general(X, Q[t * TILE:(t + 1) * TILE, :], (((1,), (1,)), ((), ())),
                                preferred_element_type=F32)
            S[:, t * TILE:(t + 1) * TILE] = s
            for j in range(TILE // 128):
                mx = jnp.maximum(mx, s[:, j * 128:(j + 1) * 128])
        XC[...] = X
        return jnp.max(mx, axis=1, keepdims=True)

    def partial(m, positive_rows, mid):
        total = jnp.zeros((ROWS, 128), F32)
        for t in range(KEYS // TILE):
            if t == 4:
                for f in mid:
                    f()
            e = jnp.exp2((S[:, t * TILE:(t + 1) * TILE] - m) * EXP2)
            for j in range(TILE // 128):
                total = total + e[:, j * 128:(j + 1) * 128]
            d = jnp.dot(e.astype(BF16), Q[t * TILE:(t + 1) * TILE, :], preferred_element_type=F32)
            if t == 0:
                ACC[...] = d
            else:
                ACC[...] += d
        l = jnp.sum(total, axis=1, keepdims=True)
        R = jnp.concatenate([p() for p in positive_rows], axis=0)
        ps = jnp.sum(XC[...].astype(F32) * R.astype(F32), axis=1, keepdims=True)
        return jnp.where(lane == 0, m, jnp.where(lane == 1, l, ps)).T

    def scores_a(zs, mid):
        return scores([lambda d=d: GA[:, zi(d)].reshape(64, D) for d in zs], mid)

    def partial_a(m, zs, mid):
        stats = partial(m, [lambda d=d: QP[:, zi(d), 0:16].reshape(64, D) for d in zs], mid)
        for n, d in enumerate(zs):
            OA[:, zi(d)] = ACC[n * 64:(n + 1) * 64].reshape(NY, 16, D)
            for r in range(3):
                SA[pl.ds(r * NZ + zi(d), 1), 0:64] = stats[r:r + 1, n * 64:(n + 1) * 64]

    def scores_b(ys, mid):
        return scores([lambda d=d: GB[yi(d)].reshape(128, D) for d in ys], mid)

    def partial_b(m, ys, mid):
        stats = partial(m, [lambda d=d: QP[yi(d), :, 16:32].reshape(128, D) for d in ys], mid)
        for n, d in enumerate(ys):
            OB[yi(d)] = ACC[n * 128:(n + 1) * 128].reshape(NZ, 16, D)
            for r in range(3):
                SB[pl.ds(r * NY + yi(d), 1), :] = stats[r:r + 1, n * 128:(n + 1) * 128]

    SA[...] = jnp.zeros_like(SA)
    SB[...] = jnp.zeros_like(SB)
    first_a, second_a = (0, 1, -1, 2), (-2, 3, -3, 4)

    def combine(ref, n, h):
        parts = [ref[i] for i in range(n)]
        top = functools.reduce(jnp.maximum, [p[0:h] for p in parts])
        total = sum(p[h:2 * h] * jnp.exp2((p[0:h] - top) * EXP2) for p in parts)
        positive = sum(p[2 * h:3 * h] for p in parts)
        return top, total, positive

    class Stats:
        def __init__(self, own, ys, mid, zs, h):
            self.own, self.ys, self.mid, self.zs, self.h = own, ys, mid, zs, h
            ys[y] = own[...]
            self.cps = [start(own, ys.at[y], ydev(d)) for d in (1, 2, 3)]

        def step(self):
            got(self.cps)
            h, mid, zs = self.h, self.mid, self.zs
            top, total, positive = combine(self.ys, NY, h)
            mid[0:h], mid[h:2 * h], mid[2 * h:3 * h] = top, total, positive
            zs[z] = mid[...]
            self.cps = [start(mid, zs.at[z], zdev(d)) for d in range(1, NZ)]

        def end(self, row, at):
            got(self.cps)
            h = self.h
            top, total, positive = combine(self.zs, NZ, h)
            w = jnp.exp2((self.own[0:h] - top) * EXP2) / total
            LS[0:h] = jnp.log(total) + (top - positive) * SIM
            for i in range(h):
                WC[i] = jnp.broadcast_to(w[i:i + 1], (128, 128)).T
            return pltpu.roll(jnp.broadcast_to(LS[pl.ds(row, 1), :], (8, 128)), at % 128, 1)[0:1]

    def scale_a(i, carry):
        w = WC[i, 0:64].reshape(NY, 16, 128)
        for j in range(D // 128):
            n = slice(j * 128, (j + 1) * 128)
            OA[:, i, :, n] = OA[:, i, :, n] * w - QP[:, i, 0:16, n].astype(F32)
        return carry

    def scale_b(i, carry):
        w = WC[i].reshape(NZ, 16, 128)
        for j in range(D // 128):
            n = slice(j * 128, (j + 1) * 128)
            OB[i, :, :, n] = OB[i, :, :, n] * w - QP[i, :, 16:32, n].astype(F32)
        return carry

    class Ring:
        def __init__(self, n, me, dev, get, sr, sl, rr, rl):
            self.n, self.h, self.me, self.dev, self.get = n, n // 2, me, dev, get
            self.sr, self.sl, self.rr, self.rl = sr, sl, rr, rl
            self.s, self.pair = 0, None

        def step(self):
            n, h = self.n, self.h
            self.s += 1
            s = self.s
            dr, dl = (self.me + h + 1 - s) % n, (self.me + n - h - 1 + s) % n
            sr, sl, rr, rl = (r.at[s - 1] for r in (self.sr, self.sl, self.rr, self.rl))
            if s == 1:
                sr[..., :HALF] = self.get(dr)[..., :HALF]
                sl[..., HALF:] = self.get(dl)[..., HALF:]
                sr, rr = (r.at[..., :HALF] for r in (sr, rr))
                sl, rl = (r.at[..., HALF:] for r in (sl, rl))
            else:
                got(self.pair)
                pr, plf = self.rr.at[s - 2], self.rl.at[s - 2]
                if s == 2:
                    sr[..., :HALF] = self.get(dr)[..., :HALF] + pr[..., :HALF]
                    sr[..., HALF:] = self.get(dr)[..., HALF:]
                    sl[..., :HALF] = self.get(dl)[..., :HALF]
                    sl[..., HALF:] = self.get(dl)[..., HALF:] + plf[..., HALF:]
                else:
                    sr[...] = self.get(dr) + pr[...]
                    sl[...] = self.get(dl) + plf[...]
            self.pair = (start(sr, rr, self.dev(1)), start(sl, rl, self.dev(-1)))

        def end(self):
            got(self.pair)
            return self.get(self.me) + self.rr[self.h - 1] + self.rl[self.h - 1]

    class Pair:
        def __init__(self, one, two):
            self.rings = (one, two)

        def step(self):
            for r in self.rings:
                r.step()

        def end(self, ref):
            one, two = self.rings
            n = ref.shape[0] // 2
            ref[0:n] = one.end()
            ref[n:] = two.end()

    first_b, second_b = (0, 1), (-1, 2)
    gb.step()
    gw = ZFirst(GW)
    pool_step(2)
    m = scores_b(first_b, [ga.step])
    gw.step()
    pass_x(1)
    partial_b(m, first_b, [lambda: pool_step(3)])
    gb.end()
    gw.step()
    m = scores_b(second_b, [])
    gw.step()
    pass_x(2)
    partial_b(m, second_b, [])
    tb = Stats(SB, SBY, SBC, SBZ, NY)
    gp.end()
    along_x(4)
    cs.append(start(GP, PALL.at[b], core))
    ga.end()
    gw.step()
    m = scores_a(first_a, [tb.step])
    pass_x(2)
    partial_a(m, first_a, [])
    loss_o[0:1, 16:32] = tb.end(y, 144 - z * 16)[:, 16:32]
    lax.fori_loop(0, NY, scale_b, 0)
    rb = Pair(
        Ring(NY, y, ydev, lambda d: OB[d, 0:4], *(r.at[:, 0:4] for r in (SBR, SBL, RBR, RBL))),
        Ring(NY, y, ydev, lambda d: OB[d, 4:8], *(r.at[:, 4:8] for r in (SBR, SBL, RBR, RBL))))
    rb.step()
    gw.step()
    m = scores_a(second_a, [])
    pass_x(2)
    partial_a(m, second_a, [rb.step])
    ta = Stats(SA, SAY, SAC, SAZ, NZ)
    gw.end()
    wcopy = start(GW, WH.at[c], core)
    pass_x(1)
    ta.step()

    wcopy.wait_recv()

    def unpack(i, carry):
        own = GW[i // NZ, i % NZ].astype(F32)
        other = WH[1 - c, i // NZ, i % NZ].astype(F32)
        at = pl.multiple_of(i * 24, 8)
        for h in range(2):
            part = jnp.where(c == h, own, other)
            n = slice(h * HALF, (h + 1) * HALF)
            WF[pl.ds(at, 16), n] = part[:, :HALF]
            WF[pl.ds(at + 16, 8), n] = part[0:8, HALF:]
        return carry

    lax.fori_loop(0, NY * NZ, unpack, 0)
    WB[...] = WF[...].astype(BF16)
    loss_o[0:1, 0:16] = ta.end(z, 128 - y * 16)[:, 0:16]
    lax.fori_loop(0, NZ, scale_a, 0)
    ra = Pair(
        Ring(NZ, z, zdev, lambda d: OA[0:2, d], *(r.at[:, 0:2] for r in (SAR, SAL, RAR, RAL))),
        Ring(NZ, z, zdev, lambda d: OA[2:4, d], *(r.at[:, 2:4] for r in (SAR, SAL, RAR, RAL))))
    ra.step()
    own_pool = pltpu.make_async_copy(GP, PALL.at[b], lsem.at[1])
    own_pool.start()

    def keys(i, carry):
        for p in range(NY):
            KV[i, p * 128:(p + 1) * 128, :] = jnp.dot(
                PALL[i, p].reshape(128, D), WB[...], preferred_element_type=F32).astype(BF16)
        return carry

    ra.step()
    rb.end(TB)
    rc = Ring(NZ, z, zdev, lambda d: TB[d], SCR, SCL, RCR, RCL)
    rc.step()
    got(passed)
    cs.extend(start(PALL.at[p], PALL.at[p], core) for p in (left, right, far))
    own_pool.wait()
    ra.step()
    rc.step()
    got(cs)
    lax.fori_loop(0, 4, keys, 0)
    ra.step()
    rc.step()
    lax.fori_loop(4, 8, keys, 0)
    out_keys = pltpu.make_async_copy(KV, keys_o, lsem.at[1])
    out_keys.start()
    rc.step()
    ra.end(TA)
    YA[y] = TA[y]
    ya = [start(TA.at[yi(d)], YA.at[y], ydev(d)) for d in (1, 2, 3)]
    grad_o[16:32] = rc.end() * SIM
    got(ya)
    grad_o[0:16] = (YA[0] + YA[1] + YA[2] + YA[3]) * SIM
    for cp in pending:
        cp.wait_send()
    out_keys.wait()


def any_spec():
    return pl.BlockSpec(memory_space=pl.ANY)


def vmem_spec():
    return pl.BlockSpec(memory_space=pltpu.VMEM)


NSEM = 192


def run_main(queries, pooled, pos, wq, wk, queue):
    z4, y2 = (4, NY, 16, D), (2, NZ, 16, D)
    grid = (NY, NZ, 16, D)
    scratch = [pltpu.VMEM((KEYS, D), BF16)] + [pltpu.VMEM(grid, BF16)] * 4
    scratch += [
        pltpu.VMEM((NY, 8, 128), jnp.int32), pltpu.VMEM((8, 128), jnp.int32), pltpu.VMEM((NZ, 8, 128), jnp.int32),
        pltpu.VMEM((ROWS, D), BF16), pltpu.VMEM((ROWS, KEYS), F32),
        pltpu.VMEM((ROWS, D), F32), pltpu.VMEM(grid, F32), pltpu.VMEM(grid, F32),
        pltpu.VMEM((NY, NZ, 32, D), BF16), pltpu.VMEM((2,) + grid, BF16), pltpu.VMEM((D, D), F32),
        pltpu.VMEM((D, D), BF16), pltpu.VMEM((8, 512, D), BF16), pltpu.VMEM((8,) + grid, BF16),
        pltpu.VMEM((24, 128), F32), pltpu.VMEM((NY, 24, 128), F32), pltpu.VMEM((24, 128), F32),
        pltpu.VMEM((NZ, 24, 128), F32), pltpu.VMEM((16, 128), F32), pltpu.VMEM((NY, 16, 128), F32),
        pltpu.VMEM((16, 128), F32), pltpu.VMEM((NZ, 16, 128), F32),
        pltpu.VMEM((8, 128), F32), pltpu.VMEM((8, 128, 128), F32),
    ]
    scratch += [pltpu.VMEM(z4, F32)] * 4 + [pltpu.VMEM(y2, F32)] * 4
    scratch += [pltpu.VMEM((NY, 16, D), F32)] * 2 + [pltpu.VMEM((NZ, 16, D), F32)]
    scratch += [pltpu.VMEM((4, 16, D), F32)] * 4
    scratch += [pltpu.SemaphoreType.DMA((NSEM,)), pltpu.SemaphoreType.DMA((NSEM,)), pltpu.SemaphoreType.DMA((2,))]
    return pl.pallas_call(
        main_kernel,
        name="retrieval",
        out_shape=[
            jax.ShapeDtypeStruct((1, 32), F32), jax.ShapeDtypeStruct((32, D), F32),
            jax.ShapeDtypeStruct((24, D), F32), jax.ShapeDtypeStruct((8, 512, D), BF16),
        ],
        in_specs=[vmem_spec()] * 5 + [any_spec()],
        out_specs=[vmem_spec()] * 3 + [any_spec()],
        scratch_shapes=scratch,
        compiler_params=pltpu.CompilerParams(
            collective_id=0, has_side_effects=True, vmem_limit_bytes=60 * 2**20),
        cost_estimate=pl.CostEstimate(flops=20 * 10**9, bytes_accessed=32 * 10**6, transcendentals=4 * 10**6),
    )(queries, pooled, pos, wq, wk, queue)


BLK = 512
WIN = BLK + 16


def enqueue_kernel(shift_ref, queue, keys, *refs):
    small, (nq, *out), (BUF, WV, isem, osem, ksem, ssem) = refs[:3], refs[3:7], refs[7:]
    passing = [pltpu.make_async_copy(small[i], out[i], ssem.at[i]) for i in range(3)]
    for cp in passing:
        cp.start()
    shift = shift_ref[0]
    steps = KEYS // BLK

    def block(i):
        rows = pl.ds(i * BLK, BLK)
        at = i * BLK + shift
        base = pl.multiple_of(jnp.clip(at // 16 * 16, 0, KEYS - WIN), 16)
        return (at, base, (at > -BLK) & (at < KEYS),
                pltpu.make_async_copy(queue.at[rows, :], BUF.at[i], isem.at[i]),
                pltpu.make_async_copy(BUF.at[i], nq.at[rows, :], osem.at[i]),
                pltpu.make_async_copy(keys.at[pl.ds(base, WIN), :], WV.at[i], ksem.at[i]))

    for i in range(steps):
        _, _, lands, load, _, fetch = block(i)
        load.start()

        @pl.when(lands)
        def _():
            fetch.start()

    for i in range(steps):
        at, base, lands, load, store, fetch = block(i)
        load.wait()

        @pl.when(lands)
        def _():
            fetch.wait()
            new = pltpu.roll(WV[i].astype(F32), (2 * WIN + base - at) % WIN, 0)[:BLK]
            row = lax.broadcasted_iota(jnp.int32, (BLK, 1), 0) + at
            ok = (row >= 0) & (row < KEYS)
            BUF[i] = jnp.where(ok, new, BUF[i].astype(F32)).astype(BF16)

        store.start()
    for i in range(steps):
        block(i)[4].wait()
    for cp in passing:
        cp.wait()


def run_enqueue(shift, queue, keys, *small):
    steps = KEYS // BLK
    return pl.pallas_call(
        enqueue_kernel,
        name="enqueue",
        out_shape=[jax.ShapeDtypeStruct((KEYS, D), BF16)]
        + [jax.ShapeDtypeStruct(a.shape, a.dtype) for a in small],
        in_specs=[pl.BlockSpec(memory_space=pltpu.SMEM)] + [any_spec()] * 2 + [vmem_spec()] * 3,
        out_specs=[any_spec()] * 4,
        scratch_shapes=[pltpu.VMEM((steps, BLK, D), BF16), pltpu.VMEM((steps, WIN, D), BF16)]
        + [pltpu.SemaphoreType.DMA((steps,))] * 3 + [pltpu.SemaphoreType.DMA((3,))],
        compiler_params=pltpu.CompilerParams(vmem_limit_bytes=60 * 2**20),
    )(shift, queue, keys, *small)


def local(queries, positives, queue, pointer, pooled, query_projection_weight, key_weight):
    loss, grad, refreshed, keys = run_main(
        queries, pooled, positives.reshape(1, 32), query_projection_weight, key_weight, queue)
    first_row = lax.axis_index("queue") * KEYS
    shift = (first_row - pointer + KEYS * NY * NZ) % (KEYS * NY * NZ)
    shift = jnp.where(shift >= KEYS, shift - KEYS * NY * NZ, shift)
    new_queue, loss, grad, refreshed = run_enqueue(
        shift, queue, keys.reshape(KEYS, D), loss, grad, refreshed)
    return loss.reshape(32), grad, new_queue, refreshed


def solution(mesh):
    both = P(("batch", "queue"), None)
    one = P("queue", None)
    return jax.shard_map(
        local,
        mesh=mesh,
        in_specs=(both, P(("batch", "queue")), one, P(), both, one, one),
        out_specs=(P(("batch", "queue")), both, one, one),
        check_vma=False,
    )
```

```python
import functools
import math

import jax
import jax.numpy as jnp
from jax import lax
from jax.experimental import pallas as pl
from jax.experimental.pallas import tpu as pltpu
from jax.sharding import PartitionSpec as P

F32 = jnp.float32
BF16 = jnp.bfloat16
MESH = pl.DeviceIdType.MESH
NY, NZ = 4, 8
D = 768
HALF = D // 2
KEYS = 4096
ROWS = 256
TILE = 512
SIM = 1.0 / (0.05 * math.sqrt(768))
EXP2 = SIM * math.log2(math.e)
RATE = 0.9


def main_kernel(
    q_in, pool_in, pos_in, wq_in, wk_in, queue,
    loss_o, grad_o, ref_o, keys_o,
    Q, GA, GB, GP, GW, POSY, POSC, POSZ, XC, S, ACC, OA, OB, QP, WH, WF, WB, KV, PALL,
    SA, SAY, SAC, SAZ, SB, SBY, SBC, SBZ, LS, WC,
    SAR, SAL, RAR, RAL, SBR, SBL, RBR, RBL, TA, YA, TB, SCR, SCL, RCR, RCL,
    ssem, rsem, lsem,
):
    b, k = lax.axis_index("batch"), lax.axis_index("queue")
    y, z = k // NZ, k % NZ
    x, c = b // 2, b % 2
    ids = iter(range(NSEM))

    def zi(d):
        return (z + d + NZ) % NZ

    def yi(d):
        return (y + d + NY) % NY

    def zdev(d):
        return (b, y * NZ + zi(d))

    def ydev(d):
        return (b, yi(d) * NZ + z)

    def xdev(d):
        return (((x + d + 4) % 4) * 2 + c, k)

    core = (b + 1 - 2 * c, k)
    pending = []

    def start(src, dst, dev):
        i = next(ids)
        cp = pltpu.make_async_remote_copy(
            src_ref=src, dst_ref=dst, send_sem=ssem.at[i], recv_sem=rsem.at[i],
            device_id=dev, device_id_type=MESH,
        )
        cp.start()
        pending.append(cp)
        return cp

    def got(group):
        for cp in group:
            cp.wait_recv()

    load_q = pltpu.make_async_copy(queue, Q, lsem.at[0])
    load_q.start()

    refreshed = RATE * wk_in[...] + (1.0 - RATE) * wq_in[...]
    ref_o[...] = refreshed
    low = jnp.where(c == 0, refreshed[:, :HALF], refreshed[:, HALF:])
    tail = jnp.concatenate([low[16:24], jnp.zeros((8, HALF), F32)], axis=0)
    GA[y, z] = q_in[0:16]
    GB[y, z] = q_in[16:32]
    GP[y, z] = pool_in[...]
    GW[y, z] = jnp.concatenate([low[0:16], tail], axis=1).astype(BF16)
    POSY[y] = jnp.zeros((8, 128), jnp.int32)
    POSY[y, 0:1, 0:32] = pos_in[...]

    barrier = pltpu.get_barrier_semaphore()
    peers = [zdev(d) for d in range(1, NZ)] + [ydev(d) for d in range(1, NY)]
    peers += [xdev(1), xdev(3), core]
    for dev in peers:
        pl.semaphore_signal(barrier, inc=1, device_id=dev, device_id_type=MESH)
    pl.semaphore_wait(barrier, len(peers))

    class YFirst:
        def __init__(self, ref):
            self.ref, self.s = ref, 0
            self.cps = [start(ref.at[y, z], ref.at[y, z], ydev(d)) for d in (1, 3, 2)]

        def step(self):
            got(self.cps)
            ref, s = self.ref, self.s + 1
            self.s = s
            r, l = zi(1 - s), zi(s - 1)
            if s < 4:
                self.cps = [start(ref.at[:, r], ref.at[:, r], zdev(1)),
                            start(ref.at[:, l], ref.at[:, l], zdev(-1))]
            else:
                self.cps = [start(ref.at[:, r, :, :HALF], ref.at[:, r, :, :HALF], zdev(1)),
                            start(ref.at[:, l, :, HALF:], ref.at[:, l, :, HALF:], zdev(-1))]

        def end(self):
            got(self.cps)

    class ZFirst:
        def __init__(self, ref):
            self.ref, self.s, self.cps = ref, 0, []
            self.step()

        def step(self):
            got(self.cps)
            ref, s = self.ref, self.s + 1
            self.s = s
            r, l = zi(1 - s), zi(s - 1)
            if s < 4:
                self.cps = [start(ref.at[y, r], ref.at[y, r], zdev(1)),
                            start(ref.at[y, l], ref.at[y, l], zdev(-1))]
            elif s == 4:
                self.cps = [start(ref.at[y, r, :, :HALF], ref.at[y, r, :, :HALF], zdev(1)),
                            start(ref.at[y, l, :, HALF:], ref.at[y, l, :, HALF:], zdev(-1))]
            elif s == 5:
                self.cps = [start(ref.at[y], ref.at[y], ydev(1)), start(ref.at[y], ref.at[y], ydev(-1))]
            else:
                u, d = yi(-1), yi(1)
                self.cps = [start(ref.at[u, :, :, :HALF], ref.at[u, :, :, :HALF], ydev(1)),
                            start(ref.at[d, :, :, HALF:], ref.at[d, :, :, HALF:], ydev(-1))]

        def end(self):
            got(self.cps)

    left, right, far = (((x + d) % 4) * 2 + c for d in (3, 1, 2))
    pieces, passed, cs = [], [], []

    def along_x(*offsets):
        for d in offsets:
            src, dst = GP.at[:, zi(d)], PALL.at[b, :, zi(d)]
            pieces.append((d, start(src, dst, xdev(1)), start(src, dst, xdev(-1))))

    def pass_x(n):
        for _ in range(n):
            d, up, down = pieces.pop(0)
            up.wait_recv()
            down.wait_recv()
            l, r = PALL.at[left, :, zi(d), :, :HALF], PALL.at[right, :, zi(d), :, HALF:]
            passed.append(start(l, l, xdev(1)))
            passed.append(start(r, r, xdev(-1)))

    pos_y = [start(POSY.at[y], POSY.at[y], ydev(d)) for d in (1, 2, 3)]
    gb = ZFirst(GB)
    ga = YFirst(GA)
    gp = YFirst(GP)
    got(pos_y)
    POSC[...] = jnp.zeros((8, 128), jnp.int32)
    for d in range(NY):
        POSC[d:d + 1] = POSY[d, 0:1]
    POSZ[z] = POSC[...]
    pos_z = [start(POSC, POSZ.at[z], zdev(d)) for d in range(1, NZ)]
    gb.step()
    ga.step()
    got(pos_z)
    load_q.wait()

    post = POSZ[...].reshape(64, 128).astype(F32).T - (k * KEYS).astype(F32)

    def positives(p, mid):
        col = jnp.concatenate([post[0:32, 8 * j + p:8 * j + p + 1] for j in range(8)], axis=0)
        for t in range(KEYS // TILE):
            if t == 4:
                for f in mid:
                    f()
            at = lax.broadcasted_iota(jnp.int32, (ROWS, TILE), 1) + t * TILE
            hot = jnp.where(at.astype(F32) == col, 1.0, 0.0).astype(BF16)
            d = jnp.dot(hot, Q[t * TILE:(t + 1) * TILE, :], preferred_element_type=F32)
            if t == 0:
                ACC[...] = d
            else:
                ACC[...] += d
        QP[p] = ACC[...].reshape(8, 32, D).astype(BF16)

    def pool_step(n):
        gp.step()
        if n == 0:
            along_x(0)
        else:
            along_x(n, -n)

    positives(0, [gb.step])
    gb.step()
    pool_step(0)
    positives(1, [ga.step])
    gb.step()
    positives(2, [lambda: pool_step(1)])
    ga.step()
    positives(3, [])

    lane = lax.broadcasted_iota(jnp.int32, (ROWS, 128), 1)

    def scores(parts, mid):
        X = jnp.concatenate([p() for p in parts], axis=0)
        mx = jnp.full((ROWS, 128), -3e38, F32)
        for t in range(KEYS // TILE):
            if t == 4:
                for f in mid:
                    f()
            s = lax.dot_general(X, Q[t * TILE:(t + 1) * TILE, :], (((1,), (1,)), ((), ())),
                                preferred_element_type=F32)
            S[:, t * TILE:(t + 1) * TILE] = s
            for j in range(TILE // 128):
                mx = jnp.maximum(mx, s[:, j * 128:(j + 1) * 128])
        XC[...] = X
        return jnp.max(mx, axis=1, keepdims=True)

    def partial(m, positive_rows, mid):
        total = jnp.zeros((ROWS, 128), F32)
        for t in range(KEYS // TILE):
            if t == 4:
                for f in mid:
                    f()
            e = jnp.exp2((S[:, t * TILE:(t + 1) * TILE] - m) * EXP2)
            for j in range(TILE // 128):
                total = total + e[:, j * 128:(j + 1) * 128]
            d = jnp.dot(e.astype(BF16), Q[t * TILE:(t + 1) * TILE, :], preferred_element_type=F32)
            if t == 0:
                ACC[...] = d
            else:
                ACC[...] += d
        l = jnp.sum(total, axis=1, keepdims=True)
        R = jnp.concatenate([p() for p in positive_rows], axis=0)
        ps = jnp.sum(XC[...].astype(F32) * R.astype(F32), axis=1, keepdims=True)
        return jnp.where(lane == 0, m, jnp.where(lane == 1, l, ps)).T

    def scores_a(zs, mid):
        return scores([lambda d=d: GA[:, zi(d)].reshape(64, D) for d in zs], mid)

    def partial_a(m, zs, mid):
        stats = partial(m, [lambda d=d: QP[:, zi(d), 0:16].reshape(64, D) for d in zs], mid)
        for n, d in enumerate(zs):
            OA[:, zi(d)] = ACC[n * 64:(n + 1) * 64].reshape(NY, 16, D)
            for r in range(3):
                SA[pl.ds(r * NZ + zi(d), 1), 0:64] = stats[r:r + 1, n * 64:(n + 1) * 64]

    def scores_b(ys, mid):
        return scores([lambda d=d: GB[yi(d)].reshape(128, D) for d in ys], mid)

    def partial_b(m, ys, mid):
        stats = partial(m, [lambda d=d: QP[yi(d), :, 16:32].reshape(128, D) for d in ys], mid)
        for n, d in enumerate(ys):
            OB[yi(d)] = ACC[n * 128:(n + 1) * 128].reshape(NZ, 16, D)
            for r in range(3):
                SB[pl.ds(r * NY + yi(d), 1), :] = stats[r:r + 1, n * 128:(n + 1) * 128]

    SA[...] = jnp.zeros_like(SA)
    SB[...] = jnp.zeros_like(SB)
    first_a, second_a = (0, 1, -1, 2), (-2, 3, -3, 4)

    def combine(ref, n, h):
        parts = [ref[i] for i in range(n)]
        top = functools.reduce(jnp.maximum, [p[0:h] for p in parts])
        total = sum(p[h:2 * h] * jnp.exp2((p[0:h] - top) * EXP2) for p in parts)
        positive = sum(p[2 * h:3 * h] for p in parts)
        return top, total, positive

    class Stats:
        def __init__(self, own, ys, mid, zs, h):
            self.own, self.ys, self.mid, self.zs, self.h = own, ys, mid, zs, h
            ys[y] = own[...]
            self.cps = [start(own, ys.at[y], ydev(d)) for d in (1, 2, 3)]

        def step(self):
            got(self.cps)
            h, mid, zs = self.h, self.mid, self.zs
            top, total, positive = combine(self.ys, NY, h)
            mid[0:h], mid[h:2 * h], mid[2 * h:3 * h] = top, total, positive
            zs[z] = mid[...]
            self.cps = [start(mid, zs.at[z], zdev(d)) for d in range(1, NZ)]

        def end(self, row, at):
            got(self.cps)
            h = self.h
            top, total, positive = combine(self.zs, NZ, h)
            w = jnp.exp2((self.own[0:h] - top) * EXP2) / total
            LS[0:h] = jnp.log(total) + (top - positive) * SIM
            for i in range(h):
                WC[i] = jnp.broadcast_to(w[i:i + 1], (128, 128)).T
            return pltpu.roll(jnp.broadcast_to(LS[pl.ds(row, 1), :], (8, 128)), at % 128, 1)[0:1]

    def scale_a(i, carry):
        w = WC[i, 0:64].reshape(NY, 16, 128)
        for j in range(D // 128):
            n = slice(j * 128, (j + 1) * 128)
            OA[:, i, :, n] = OA[:, i, :, n] * w - QP[:, i, 0:16, n].astype(F32)
        return carry

    def scale_b(i, carry):
        w = WC[i].reshape(NZ, 16, 128)
        for j in range(D // 128):
            n = slice(j * 128, (j + 1) * 128)
            OB[i, :, :, n] = OB[i, :, :, n] * w - QP[i, :, 16:32, n].astype(F32)
        return carry

    class Ring:
        def __init__(self, n, me, dev, get, sr, sl, rr, rl):
            self.n, self.h, self.me, self.dev, self.get = n, n // 2, me, dev, get
            self.sr, self.sl, self.rr, self.rl = sr, sl, rr, rl
            self.s, self.pair = 0, None

        def step(self):
            n, h = self.n, self.h
            self.s += 1
            s = self.s
            dr, dl = (self.me + h + 1 - s) % n, (self.me + n - h - 1 + s) % n
            sr, sl, rr, rl = (r.at[s - 1] for r in (self.sr, self.sl, self.rr, self.rl))
            if s == 1:
                sr[..., :HALF] = self.get(dr)[..., :HALF]
                sl[..., HALF:] = self.get(dl)[..., HALF:]
                sr, rr = (r.at[..., :HALF] for r in (sr, rr))
                sl, rl = (r.at[..., HALF:] for r in (sl, rl))
            else:
                got(self.pair)
                pr, plf = self.rr.at[s - 2], self.rl.at[s - 2]
                if s == 2:
                    sr[..., :HALF] = self.get(dr)[..., :HALF] + pr[..., :HALF]
                    sr[..., HALF:] = self.get(dr)[..., HALF:]
                    sl[..., :HALF] = self.get(dl)[..., :HALF]
                    sl[..., HALF:] = self.get(dl)[..., HALF:] + plf[..., HALF:]
                else:
                    sr[...] = self.get(dr) + pr[...]
                    sl[...] = self.get(dl) + plf[...]
            self.pair = (start(sr, rr, self.dev(1)), start(sl, rl, self.dev(-1)))

        def end(self):
            got(self.pair)
            return self.get(self.me) + self.rr[self.h - 1] + self.rl[self.h - 1]

    class Pair:
        def __init__(self, one, two):
            self.rings = (one, two)

        def step(self):
            for r in self.rings:
                r.step()

        def end(self, ref):
            one, two = self.rings
            n = ref.shape[0] // 2
            ref[0:n] = one.end()
            ref[n:] = two.end()

    first_b, second_b = (0, 1), (-1, 2)
    gb.step()
    gw = ZFirst(GW)
    pool_step(2)
    m = scores_b(first_b, [ga.step])
    gw.step()
    pass_x(1)
    partial_b(m, first_b, [lambda: pool_step(3)])
    gb.end()
    gw.step()
    m = scores_b(second_b, [])
    gw.step()
    pass_x(2)
    partial_b(m, second_b, [])
    tb = Stats(SB, SBY, SBC, SBZ, NY)
    gp.end()
    along_x(4)
    cs.append(start(GP, PALL.at[b], core))
    ga.end()
    gw.step()
    m = scores_a(first_a, [tb.step])
    pass_x(2)
    partial_a(m, first_a, [])
    loss_o[0:1, 16:32] = tb.end(y, 144 - z * 16)[:, 16:32]
    lax.fori_loop(0, NY, scale_b, 0)
    rb = Pair(
        Ring(NY, y, ydev, lambda d: OB[d, 0:4], *(r.at[:, 0:4] for r in (SBR, SBL, RBR, RBL))),
        Ring(NY, y, ydev, lambda d: OB[d, 4:8], *(r.at[:, 4:8] for r in (SBR, SBL, RBR, RBL))))
    rb.step()
    gw.step()
    m = scores_a(second_a, [])
    pass_x(2)
    partial_a(m, second_a, [rb.step])
    ta = Stats(SA, SAY, SAC, SAZ, NZ)
    ta.step()

    loss_o[0:1, 0:16] = ta.end(z, 128 - y * 16)[:, 0:16]
    lax.fori_loop(0, NZ, scale_a, 0)
    ra = Pair(
        Ring(NZ, z, zdev, lambda d: OA[0:2, d], *(r.at[:, 0:2] for r in (SAR, SAL, RAR, RAL))),
        Ring(NZ, z, zdev, lambda d: OA[2:4, d], *(r.at[:, 2:4] for r in (SAR, SAL, RAR, RAL))))
    ra.step()
    gw.end()
    wcopy = start(GW, WH.at[c], core)
    pass_x(1)
    own_pool = pltpu.make_async_copy(GP, PALL.at[b], lsem.at[1])
    own_pool.start()

    def keys(i, carry):
        for p in range(NY):
            KV[i, p * 128:(p + 1) * 128, :] = jnp.dot(
                PALL[i, p].reshape(128, D), WB[...], preferred_element_type=F32).astype(BF16)
        return carry

    ra.step()
    rb.end(TB)
    rc = Ring(NZ, z, zdev, lambda d: TB[d], SCR, SCL, RCR, RCL)
    rc.step()

    wcopy.wait_recv()

    def unpack(i, carry):
        own = GW[i // NZ, i % NZ].astype(F32)
        other = WH[1 - c, i // NZ, i % NZ].astype(F32)
        at = pl.multiple_of(i * 24, 8)
        for h in range(2):
            part = jnp.where(c == h, own, other)
            n = slice(h * HALF, (h + 1) * HALF)
            WF[pl.ds(at, 16), n] = part[:, :HALF]
            WF[pl.ds(at + 16, 8), n] = part[0:8, HALF:]
        return carry

    lax.fori_loop(0, NY * NZ, unpack, 0)
    WB[...] = WF[...].astype(BF16)
    got(passed)
    cs.extend(start(PALL.at[p], PALL.at[p], core) for p in (left, right, far))
    own_pool.wait()
    ra.step()
    rc.step()
    got(cs)
    lax.fori_loop(0, 4, keys, 0)
    ra.step()
    rc.step()
    lax.fori_loop(4, 8, keys, 0)
    out_keys = pltpu.make_async_copy(KV, keys_o, lsem.at[1])
    out_keys.start()
    rc.step()
    ra.end(TA)
    YA[y] = TA[y]
    ya = [start(TA.at[yi(d)], YA.at[y], ydev(d)) for d in (1, 2, 3)]
    grad_o[16:32] = rc.end() * SIM
    got(ya)
    grad_o[0:16] = (YA[0] + YA[1] + YA[2] + YA[3]) * SIM
    for cp in pending:
        cp.wait_send()
    out_keys.wait()


def any_spec():
    return pl.BlockSpec(memory_space=pl.ANY)


def vmem_spec():
    return pl.BlockSpec(memory_space=pltpu.VMEM)


NSEM = 192


def run_main(queries, pooled, pos, wq, wk, queue):
    z4, y2 = (4, NY, 16, D), (2, NZ, 16, D)
    grid = (NY, NZ, 16, D)
    scratch = [pltpu.VMEM((KEYS, D), BF16)] + [pltpu.VMEM(grid, BF16)] * 4
    scratch += [
        pltpu.VMEM((NY, 8, 128), jnp.int32), pltpu.VMEM((8, 128), jnp.int32), pltpu.VMEM((NZ, 8, 128), jnp.int32),
        pltpu.VMEM((ROWS, D), BF16), pltpu.VMEM((ROWS, KEYS), F32),
        pltpu.VMEM((ROWS, D), F32), pltpu.VMEM(grid, F32), pltpu.VMEM(grid, F32),
        pltpu.VMEM((NY, NZ, 32, D), BF16), pltpu.VMEM((2,) + grid, BF16), pltpu.VMEM((D, D), F32),
        pltpu.VMEM((D, D), BF16), pltpu.VMEM((8, 512, D), BF16), pltpu.VMEM((8,) + grid, BF16),
        pltpu.VMEM((24, 128), F32), pltpu.VMEM((NY, 24, 128), F32), pltpu.VMEM((24, 128), F32),
        pltpu.VMEM((NZ, 24, 128), F32), pltpu.VMEM((16, 128), F32), pltpu.VMEM((NY, 16, 128), F32),
        pltpu.VMEM((16, 128), F32), pltpu.VMEM((NZ, 16, 128), F32),
        pltpu.VMEM((8, 128), F32), pltpu.VMEM((8, 128, 128), F32),
    ]
    scratch += [pltpu.VMEM(z4, F32)] * 4 + [pltpu.VMEM(y2, F32)] * 4
    scratch += [pltpu.VMEM((NY, 16, D), F32)] * 2 + [pltpu.VMEM((NZ, 16, D), F32)]
    scratch += [pltpu.VMEM((4, 16, D), F32)] * 4
    scratch += [pltpu.SemaphoreType.DMA((NSEM,)), pltpu.SemaphoreType.DMA((NSEM,)), pltpu.SemaphoreType.DMA((2,))]
    return pl.pallas_call(
        main_kernel,
        name="retrieval",
        out_shape=[
            jax.ShapeDtypeStruct((1, 32), F32), jax.ShapeDtypeStruct((32, D), F32),
            jax.ShapeDtypeStruct((24, D), F32), jax.ShapeDtypeStruct((8, 512, D), BF16),
        ],
        in_specs=[vmem_spec()] * 5 + [any_spec()],
        out_specs=[vmem_spec()] * 3 + [any_spec()],
        scratch_shapes=scratch,
        compiler_params=pltpu.CompilerParams(
            collective_id=0, has_side_effects=True, vmem_limit_bytes=60 * 2**20),
        cost_estimate=pl.CostEstimate(flops=20 * 10**9, bytes_accessed=32 * 10**6, transcendentals=4 * 10**6),
    )(queries, pooled, pos, wq, wk, queue)


BLK = 512
WIN = BLK + 16


def enqueue_kernel(shift_ref, queue, keys, *refs):
    small, (nq, *out), (BUF, WV, isem, osem, ksem, ssem) = refs[:3], refs[3:7], refs[7:]
    passing = [pltpu.make_async_copy(small[i], out[i], ssem.at[i]) for i in range(3)]
    for cp in passing:
        cp.start()
    shift = shift_ref[0]
    steps = KEYS // BLK

    def block(i):
        rows = pl.ds(i * BLK, BLK)
        at = i * BLK + shift
        base = pl.multiple_of(jnp.clip(at // 16 * 16, 0, KEYS - WIN), 16)
        return (at, base, (at > -BLK) & (at < KEYS),
                pltpu.make_async_copy(queue.at[rows, :], BUF.at[i], isem.at[i]),
                pltpu.make_async_copy(BUF.at[i], nq.at[rows, :], osem.at[i]),
                pltpu.make_async_copy(keys.at[pl.ds(base, WIN), :], WV.at[i], ksem.at[i]))

    for i in range(steps):
        _, _, lands, load, _, fetch = block(i)
        load.start()

        @pl.when(lands)
        def _():
            fetch.start()

    for i in range(steps):
        at, base, lands, load, store, fetch = block(i)
        load.wait()

        @pl.when(lands)
        def _():
            fetch.wait()
            new = pltpu.roll(WV[i].astype(F32), (2 * WIN + base - at) % WIN, 0)[:BLK]
            row = lax.broadcasted_iota(jnp.int32, (BLK, 1), 0) + at
            ok = (row >= 0) & (row < KEYS)
            BUF[i] = jnp.where(ok, new, BUF[i].astype(F32)).astype(BF16)

        store.start()
    for i in range(steps):
        block(i)[4].wait()
    for cp in passing:
        cp.wait()


def run_enqueue(shift, queue, keys, *small):
    steps = KEYS // BLK
    return pl.pallas_call(
        enqueue_kernel,
        name="enqueue",
        out_shape=[jax.ShapeDtypeStruct((KEYS, D), BF16)]
        + [jax.ShapeDtypeStruct(a.shape, a.dtype) for a in small],
        in_specs=[pl.BlockSpec(memory_space=pltpu.SMEM)] + [any_spec()] * 2 + [vmem_spec()] * 3,
        out_specs=[any_spec()] * 4,
        scratch_shapes=[pltpu.VMEM((steps, BLK, D), BF16), pltpu.VMEM((steps, WIN, D), BF16)]
        + [pltpu.SemaphoreType.DMA((steps,))] * 3 + [pltpu.SemaphoreType.DMA((3,))],
        compiler_params=pltpu.CompilerParams(vmem_limit_bytes=60 * 2**20),
    )(shift, queue, keys, *small)


def local(queries, positives, queue, pointer, pooled, query_projection_weight, key_weight):
    loss, grad, refreshed, keys = run_main(
        queries, pooled, positives.reshape(1, 32), query_projection_weight, key_weight, queue)
    first_row = lax.axis_index("queue") * KEYS
    shift = (first_row - pointer + KEYS * NY * NZ) % (KEYS * NY * NZ)
    shift = jnp.where(shift >= KEYS, shift - KEYS * NY * NZ, shift)
    new_queue, loss, grad, refreshed = run_enqueue(
        shift, queue, keys.reshape(KEYS, D), loss, grad, refreshed)
    return loss.reshape(32), grad, new_queue, refreshed


def solution(mesh):
    both = P(("batch", "queue"), None)
    one = P("queue", None)
    return jax.shard_map(
        local,
        mesh=mesh,
        in_specs=(both, P(("batch", "queue")), one, P(), both, one, one),
        out_specs=(P(("batch", "queue")), both, one, one),
        check_vma=False,
    )
```
